32 devices in a mesh: basis: 4 (over y, core), dp: 8 (over z, x).
Axes of the slice: x: 2, y: 2, z: 4, core: 2. Of those that a mesh axis runs over, the one named last changes fastest.
Arguments:
- gradient: bfloat16 [2048, 8192], P('basis', 'dp'), may hold values from -6 to 6
- left_basis: float32 [2048, 2048], P('basis', 'dp'), may hold values from -0.125 to 0.125
- right_basis: float32 [8192, 8192], P('basis', 'dp'), may hold values from -0.0625 to 0.0625
- first_moment: float32 [2048, 8192], P('basis', 'dp'), may hold values from -1.5 to 1.5
- second_moment: float32 [2048, 8192], P('basis', 'dp'), may hold values from 0.04 to 1
Outputs:
- first_new: float32 [2048, 8192], P('basis', 'dp')
- second_new: float32 [2048, 8192], P('basis', 'dp')
- update: bfloat16 [2048, 8192], P('dp', 'basis')
The draws below stay inside these ranges and needn't reach their ends.
All inputs are finite; a program needn't handle non-finite values.
Results may differ from the reference program's by a relative error of at most 0.018.
Values may be sent and summed in bfloat16 or wider, within the bound.
No kernel may reach another device: no remote copies, remote signals or barrier semaphores. Data moves between devices by JAX's collectives and lax.ppermute only.
A program may use at most 128 MiB of HBM per device.

```python
import math
import jax
import jax.numpy as jnp
from jax import lax

D = 2048
FF = 8192
STEP = 4
GROUPS_B = 4
GROUPS_D = 8


def steps_of(rng, extent, pieces, low, top_value):
    level, own = 1.0, jax.random.fold_in(rng, 6)
    for position, shards_of in pieces:
        heights = jnp.exp(jax.random.uniform(jax.random.fold_in(own, position), (shards_of,), jnp.float32, low / len(pieces), top_value / len(pieces)))
        level = level * jnp.repeat(heights, extent[position] // shards_of).reshape([-1 if axis == position else 1 for axis in range(len(extent))])
    return level


def centred(own_key, extent, deviation, reach, shards=(), held_as=jnp.bfloat16):
    gain = steps_of(own_key, extent, shards, -0.22, 0.18) if shards else 1.0
    entries = jax.random.normal(own_key, extent, jnp.float32) * deviation * gain
    return jnp.minimum(jnp.maximum(entries, -reach), reach).astype(held_as)


def setup_inputs(seed: int = 0) -> dict:
    key_of = jax.random.split(jax.random.key(seed), 6)
    return {
        "gradient": centred(key_of[0], (D, FF), 1.0, 6.0, ((0, 4), (1, 8))),
        "left_basis": centred(key_of[1], (D, D), D ** -0.5, 0.125, ((0, 4), (1, 8)), jnp.float32),
        "right_basis": centred(key_of[2], (FF, FF), FF ** -0.5, 0.0625, ((0, 4), (1, 8)), jnp.float32),
        "first_moment": centred(key_of[3], (D, FF), 0.1, 1.5, ((0, 4), (1, 8)), jnp.float32),
        "second_moment": jnp.clip(jnp.exp(math.log(1.0) - 3.218876 * jax.random.uniform(key_of[4], (D, FF), jnp.float32) ** steps_of(key_of[4], (D, FF), ((0, 4), (1, 8)), -0.2, 0.2)), 0.04, 1.0),
    }


beta_first = 0.95
beta_second = 0.95
epsilon = 1e-08

def rounded(value):
    low = value.astype(jnp.bfloat16)
    low = lax.optimization_barrier(low)
    return low.astype(jnp.float32)

def reference(gradient, left_basis, right_basis, first_moment, second_moment):
    rows_block = D // GROUPS_B
    grad_wide = gradient.astype(jnp.float32)

    def left_step(total, index):
        start = index * rows_block
        basis_part = lax.dynamic_slice_in_dim(left_basis, start, rows_block, 0)
        grad_part = lax.dynamic_slice_in_dim(grad_wide, start, rows_block, 0)
        term_value = lax.dot_general(basis_part, grad_part, (((0,), (0,)), ((), ())), precision=lax.Precision.HIGHEST, preferred_element_type=jnp.float32)
        return (total + rounded(term_value), None)
    left_sum, _ = lax.scan(left_step, jnp.zeros((D, FF), jnp.float32), jnp.arange(GROUPS_B, dtype=jnp.int32))
    rotated_left = rounded(left_sum)
    right_block = FF // GROUPS_B

    def right_step(total, index):
        start = index * right_block
        left_part = lax.dynamic_slice_in_dim(rotated_left, start, right_block, 1)
        basis_part = lax.dynamic_slice_in_dim(right_basis, start, right_block, 0)
        term_value = jnp.dot(left_part, basis_part, precision=lax.Precision.HIGHEST, preferred_element_type=jnp.float32)
        return (total + rounded(term_value), None)
    rotated, _ = lax.scan(right_step, jnp.zeros((D, FF), jnp.float32), jnp.arange(GROUPS_B, dtype=jnp.int32))
    first_new = beta_first * first_moment + (1.0 - beta_first) * rotated
    second_new = beta_second * second_moment + (1.0 - beta_second) * rotated * rotated
    first_fix = 1.0 - beta_first ** STEP
    second_fix = 1.0 - beta_second ** STEP
    direction = first_new / first_fix / (jnp.sqrt(second_new / second_fix) + epsilon)
    direction_low = rounded(direction)
    back_left = rounded(jnp.dot(left_basis, direction_low, precision=lax.Precision.HIGHEST, preferred_element_type=jnp.float32))
    column_block = FF // GROUPS_D

    def back_step(total, index):
        start = index * column_block
        back_part = lax.dynamic_slice_in_dim(back_left, start, column_block, 1)
        basis_part = lax.dynamic_slice_in_dim(right_basis, start, column_block, 1)
        term_value = lax.dot_general(back_part, basis_part, (((1,), (1,)), ((), ())), precision=lax.Precision.HIGHEST, preferred_element_type=jnp.float32)
        return (total + rounded(term_value), None)
    update, _ = lax.scan(back_step, jnp.zeros((D, FF), jnp.float32), jnp.arange(GROUPS_D, dtype=jnp.int32))
    return (first_new, second_new, update.astype(jnp.bfloat16))
```

```python
import jax
import jax.numpy as jnp
from jax import lax
from jax.sharding import PartitionSpec as P

STEP = 4


beta_first = 0.95
beta_second = 0.95
epsilon = 1e-08

CHUNKS = 2

BOTH = ("basis", "dp")


def matmul(a, b, contract):
    return lax.dot_general(a, b, (contract, ((), ())), preferred_element_type=jnp.float32)


def per_device(gradient, left_basis, right_basis, first_moment, second_moment, *, nb, nd):
    nz = nb
    nx = nd // nz
    b = lax.axis_index("basis")
    d = lax.axis_index("dp")
    z, x = d // nx, d % nx
    low = jnp.bfloat16

    def spread(beta):
        return (beta >> 1) ^ ((beta & 1) * (nz - 1))

    unspread = {spread(beta): beta for beta in range(nb)}

    def permute(value, target):
        pairs = []
        for bb in range(nb):
            for zz in range(nz):
                for xx in range(nx):
                    tb, tz, tx = target(bb, zz, xx)
                    pairs.append((bb * nd + zz * nx + xx, tb * nd + tz * nx + tx))
        return lax.ppermute(value, BOTH, pairs)

    ff_block = right_basis.shape[1]
    rows = first_moment.shape[0]
    out_rows = left_basis.shape[1]

    left_rows = lax.all_gather(left_basis.astype(low), "dp", axis=1, tiled=True)
    left = lax.all_gather(left_rows, "basis", axis=0, tiled=True)

    right = right_basis.astype(low)
    right_part = [lax.dynamic_slice_in_dim(right_basis, (x ^ u) * ff_block, ff_block, 0).astype(low) for u in range(nx)]

    half = jnp.zeros((rows * nb, ff_block), low)
    for s in range(nb):
        piece = permute(gradient, lambda bb, zz, xx: (bb, zz ^ spread(bb) ^ s, xx))
        piece = permute(piece, lambda bb, zz, xx: (zz ^ spread(bb) ^ s, zz, xx))
        total = matmul(piece, right_part[0], ((1,), (0,)))
        for u in range(1, nx):
            other = permute(piece, lambda bb, zz, xx: (bb, zz, xx ^ u))
            total = total + matmul(other, right_part[u], ((1,), (0,)))
        source = jnp.array([unspread[i] for i in range(nb)], jnp.int32)[b ^ z ^ s]
        half = lax.dynamic_update_slice_in_dim(half, total.astype(low), source * rows, 0)

    order = list(range(0, nb, 2)) + list(range(1, nb, 2))
    left_cols = jnp.concatenate(
        [lax.dynamic_slice_in_dim(left, (b ^ t) * rows, rows, 1) for t in order], axis=1
    )
    left_out = jnp.concatenate(
        [
            lax.dynamic_slice_in_dim(left_cols, ((z ^ spread_of(b, nz) ^ s) * nx + (x ^ u)) * out_rows, out_rows, 0)
            for s in range(nz)
            for u in range(nx)
        ],
        axis=0,
    )

    width = ff_block // CHUNKS
    first_out, second_out, back = [], [], []
    for j in range(CHUNKS):
        cols = slice(j * width, (j + 1) * width)
        held = {}
        mine = nb // 2 * rows
        gone = matmul(left_cols[:, mine:], half[:, cols], ((0,), (0,))).astype(low)
        got = permute(gone, lambda bb, zz, xx: (bb ^ 1, zz, xx))
        total = matmul(left_cols[:, :mine], half[:, cols], ((0,), (0,))) + got.astype(jnp.float32)
        count = nb // 2
        step = nb // 2
        bit = nb // 2
        while count > 1:
            keep = total[: count // 2 * rows]
            send = total[count // 2 * rows :].astype(low)
            got = permute(send, lambda bb, zz, xx: (bb ^ bit, zz, xx))
            total = keep + got.astype(jnp.float32)
            count //= 2
            bit //= 2
        rotated = total
        first_new = beta_first * first_moment[:, cols] + (1.0 - beta_first) * rotated
        second_new = beta_second * second_moment[:, cols] + (1.0 - beta_second) * rotated * rotated
        first_fix = 1.0 - beta_first**STEP
        second_fix = 1.0 - beta_second**STEP
        direction = first_new / first_fix / (jnp.sqrt(second_new / second_fix) + epsilon)
        first_out.append(first_new)
        second_out.append(second_new)
        column = direction.astype(low)
        bit = 2
        while bit < nb:
            column = jnp.concatenate([column, permute(column, lambda bb, zz, xx: (bb ^ bit, zz, xx))], axis=0)
            bit *= 2
        column = jnp.concatenate([column, permute(column, lambda bb, zz, xx: (bb ^ 1, zz, xx))], axis=0)
        back.append(matmul(left_out, column, ((1,), (0,))).astype(low))
    back = jnp.concatenate(back, axis=1)

    update = None
    for s in reversed(range(nz)):
        base = s * nx * out_rows
        gots = []
        for u in range(1, nx):
            rows_of = back[base + u * out_rows : base + (u + 1) * out_rows]
            sent = matmul(rows_of, right, ((1,), (1,))).astype(low)
            gots.append(permute(sent, lambda bb, zz, xx: (bb, zz, xx ^ u)))
        total = matmul(back[base : base + out_rows], right, ((1,), (1,)))
        for got in gots:
            total = total + got.astype(jnp.float32)
        got = permute(total.astype(low), lambda bb, zz, xx: (bb, zz ^ spread(bb) ^ s, xx)).astype(jnp.float32)
        update = got if update is None else update + got
    return (
        jnp.concatenate(first_out, axis=1),
        jnp.concatenate(second_out, axis=1),
        update.astype(low),
    )


def spread_of(beta, nz):
    return (beta >> 1) ^ ((beta & 1) * (nz - 1))


def solution(mesh):
    nb, nd = mesh.shape["basis"], mesh.shape["dp"]

    def run(*args):
        return per_device(*args, nb=nb, nd=nd)

    return jax.shard_map(
        run,
        mesh=mesh,
        in_specs=(
            P("basis", "dp"),
            P("basis", "dp"),
            P("basis", "dp"),
            P("basis", "dp"),
            P("basis", "dp"),
        ),
        out_specs=(P("basis", "dp"), P("basis", "dp"), P("dp", "basis")),
        check_vma=False,
    )
```

```python
import jax
import jax.numpy as jnp
from jax import lax
from jax.sharding import PartitionSpec as P

STEP = 4


beta_first = 0.95
beta_second = 0.95
epsilon = 1e-08

ROW_PARTS = 2
COL_PARTS = 2
WINDOW = 6

low = jnp.bfloat16


def matmul(a, b):
    return lax.dot_general(a, b, (((1,), (0,)), ((), ())), preferred_element_type=jnp.float32)


def matmul_nt(a, b):
    return lax.dot_general(a, b, (((1,), (1,)), ((), ())), preferred_element_type=jnp.float32)


def per_device(gradient, left_basis, right_basis, first_moment, second_moment, *, nb, nd):
    nz = nb
    nx = nd // nz
    b = lax.axis_index("basis")
    d = lax.axis_index("dp")
    z, x = d // nx, d % nx
    bits = [1 << k for k in range(nb.bit_length() - 1)]
    x_bits = [1 << k for k in range(nx.bit_length() - 1)]

    def permute(value, target):
        pairs = []
        for bb in range(nb):
            for zz in range(nz):
                for xx in range(nx):
                    tb, tz, tx = target(bb, zz, xx)
                    pairs.append((bb * nd + zz * nx + xx, tb * nd + tz * nx + tx))
        return lax.ppermute(value, ("basis", "dp"), pairs)

    def move_b(value, t):
        return permute(value, lambda bb, zz, xx: (bb ^ t, zz, xx))

    def move_z(value, t):
        return permute(value, lambda bb, zz, xx: (bb, zz ^ t, xx))

    def move_x(value, u):
        return permute(value, lambda bb, zz, xx: (bb, zz, xx ^ u))

    def spread(beta):
        return (beta >> 1) ^ ((beta & 1) * (nz - 1))

    unspread = [0] * nz
    for beta in range(nb):
        unspread[spread(beta)] = beta

    def joined(mine, other, bit_set, axis):
        first = jnp.where(bit_set, other, mine)
        second = jnp.where(bit_set, mine, other)
        return jnp.stack([first, second], axis=axis)

    ff_block = right_basis.shape[1]
    rows = first_moment.shape[0]
    out_rows = left_basis.shape[1]
    whole = rows * nb

    ended = []

    def in_turn(value):
        if len(ended) >= WINDOW:
            value, _ = lax.optimization_barrier((value, ended[-WINDOW]))
        return value

    def sent(value, move, t):
        result = move(in_turn(value), t)
        ended.append(result)
        return result

    left_t = left_basis.astype(low).T

    def left_steps():
        value = left_t
        for i, t in enumerate(reversed(bits[1:])):
            value = joined(value, sent(value, move_z, t), (z & t) != 0, i)
            yield
        for i, u in enumerate(reversed(x_bits)):
            value = joined(value, sent(value, move_x, u), (x & u) != 0, len(bits) - 1 + i)
            yield
        value = joined(value, sent(value, move_z, bits[0]), (z & bits[0]) != 0, len(bits) - 1)
        yield
        value = value.reshape(whole, rows)
        for i, t in enumerate(reversed(bits)):
            value = joined(value, sent(value, move_b, t), (b & t) != 0, 1 + i)
            yield
        left_all.append(value.reshape(whole, whole))

    left_all = []
    left_turns = left_steps()

    right = right_basis.astype(low)
    right_part = [
        lax.dynamic_slice_in_dim(right_basis, (x ^ u) * ff_block, ff_block, 0).astype(low) for u in range(nx)
    ]

    part = rows // ROW_PARTS
    half = jnp.zeros((whole, ff_block), low)
    sources = jnp.array(unspread, jnp.int32)
    next(left_turns, None)
    pieces = [gradient[h * part : (h + 1) * part] for h in range(ROW_PARTS)]
    pieces = [sent(piece, lambda v, _: permute(v, lambda bb, zz, xx: (bb, zz ^ spread(bb), xx)), 0) for piece in pieces]
    next(left_turns, None)
    pieces = [sent(piece, lambda v, _: permute(v, lambda bb, zz, xx: (zz ^ spread(bb), zz, xx)), 0) for piece in pieces]
    blocks = {(0, h): piece for h, piece in enumerate(pieces)}
    turns = sorted(range(nz), key=lambda s: (s.bit_count(), s))
    ahead = 1
    for i, s in enumerate(turns):
        for h in range(ROW_PARTS):
            others = [sent(blocks[s, h], move_x, u) for u in range(1, nx)]
            total = matmul(blocks[s, h], right_part[0])
            for u, other in enumerate(others):
                total = total + matmul(other, right_part[u + 1])
            start = sources[b ^ z ^ s] * rows + h * part
            half = lax.dynamic_update_slice_in_dim(half, total.astype(low), start, 0)
            for k in range(ahead, min(i + 3, nz)):
                t = turns[k]
                blocks[t, h] = sent(blocks[t & (t - 1), h], move_z, t & -t)
        ahead = min(i + 3, nz)
        next(left_turns, None)
    for _ in left_turns:
        pass
    left_t = left_all[0]
    left = left_t.T

    def left_t_rows(t):
        return lax.dynamic_slice_in_dim(left_t, (b ^ t) * rows, rows, 0)

    width = ff_block // COL_PARTS
    first_out, second_out, columns = [], [], []
    for j in range(COL_PARTS):
        cols = slice(j * width, (j + 1) * width)
        part_half = half[:, cols]
        gone = jnp.concatenate([matmul(left_t_rows(t), part_half).astype(low) for t in range(1, nb, 2)], axis=0)
        got = move_b(gone, 1)
        held = {}
        for i, t in enumerate(range(0, nb, 2)):
            held[t] = matmul(left_t_rows(t), part_half) + got[i * rows : (i + 1) * rows].astype(jnp.float32)
        for t in reversed(bits[1:]):
            away = [s for s in held if s & t]
            got = move_b(jnp.concatenate([held[s].astype(low) for s in away], axis=0), t)
            for i, s in enumerate(away):
                held[s ^ t] = held[s ^ t] + got[i * rows : (i + 1) * rows].astype(jnp.float32)
                del held[s]
        rotated = held[0]
        first_new = beta_first * first_moment[:, cols] + (1.0 - beta_first) * rotated
        second_new = beta_second * second_moment[:, cols] + (1.0 - beta_second) * rotated * rotated
        first_fix = 1.0 - beta_first**STEP
        second_fix = 1.0 - beta_second**STEP
        direction = first_new / first_fix / (jnp.sqrt(second_new / second_fix) + epsilon)
        first_out.append(first_new)
        second_out.append(second_new)
        column = direction.astype(low)
        axis = 0
        for t in reversed(bits):
            column = joined(column, move_b(column, t), (b & t) != 0, axis)
            axis += 1
        columns.append(column.reshape(whole, width))
    columns = jnp.concatenate(columns, axis=1)

    def partial(s, u):
        start = ((z ^ s) * nx + (x ^ u)) * out_rows
        rows_of = lax.dynamic_slice_in_dim(left, start, out_rows, 0)
        return matmul_nt(matmul(rows_of, columns).astype(low), right)

    order = sorted(range(nz), key=lambda s: tuple(-(s >> k & 1) for k in range(len(bits))))
    sums = {}
    for s in order:
        gots = [move_x(partial(s, u).astype(low), u) for u in range(1, nx)]
        total = partial(s, 0)
        for got in gots:
            total = total + got.astype(jnp.float32)
        sums[s] = total
    for t in bits:
        for s in [s for s in order if s in sums and s & t]:
            sums[s ^ t] = sums[s ^ t] + move_z(sums.pop(s).astype(low), t).astype(jnp.float32)
    return (
        jnp.concatenate(first_out, axis=1),
        jnp.concatenate(second_out, axis=1),
        sums[0].astype(low),
    )


def solution(mesh):
    nb, nd = mesh.shape["basis"], mesh.shape["dp"]

    def run(*args):
        return per_device(*args, nb=nb, nd=nd)

    return jax.shard_map(
        run,
        mesh=mesh,
        in_specs=(
            P("basis", "dp"),
            P("basis", "dp"),
            P("basis", "dp"),
            P("basis", "dp"),
            P("basis", "dp"),
        ),
        out_specs=(P("basis", "dp"), P("basis", "dp"), P("dp", "basis")),
        check_vma=False,
    )
```

```python
import jax
import jax.numpy as jnp
from jax import lax
from jax.sharding import PartitionSpec as P

STEP = 4


beta_first = 0.95
beta_second = 0.95
epsilon = 1e-08

ROW_PARTS = 2
COL_PARTS = 2
OUT_PARTS = 2

low = jnp.bfloat16


def matmul(a, b):
    return lax.dot_general(a, b, (((1,), (0,)), ((), ())), preferred_element_type=jnp.float32)


def matmul_nt(a, b):
    return lax.dot_general(a, b, (((1,), (1,)), ((), ())), preferred_element_type=jnp.float32)


def per_device(gradient, left_basis, right_basis, first_moment, second_moment, *, nb, nd):
    nz = nb
    nx = nd // nz
    b = lax.axis_index("basis")
    d = lax.axis_index("dp")
    z, x = d // nx, d % nx
    bits = [1 << k for k in range(nb.bit_length() - 1)]
    x_bits = [1 << k for k in range(nx.bit_length() - 1)]

    def permute(value, target):
        pairs = []
        for bb in range(nb):
            for zz in range(nz):
                for xx in range(nx):
                    tb, tz, tx = target(bb, zz, xx)
                    pairs.append((bb * nd + zz * nx + xx, tb * nd + tz * nx + tx))
        return lax.ppermute(value, ("basis", "dp"), pairs)

    def move_b(value, t):
        return permute(value, lambda bb, zz, xx: (bb ^ t, zz, xx))

    def move_z(value, t):
        return permute(value, lambda bb, zz, xx: (bb, zz ^ t, xx))

    def move_x(value, u):
        return permute(value, lambda bb, zz, xx: (bb, zz, xx ^ u))

    def spread(beta):
        return (beta >> 1) ^ ((beta & 1) * (nz - 1))

    unspread = [0] * nz
    for beta in range(nb):
        unspread[spread(beta)] = beta

    def joined(mine, other, bit_set, axis):
        first = jnp.where(bit_set, other, mine)
        second = jnp.where(bit_set, mine, other)
        return jnp.stack([first, second], axis=axis)

    ff_block = right_basis.shape[1]
    rows = first_moment.shape[0]
    out_rows = left_basis.shape[1]
    whole = rows * nb

    path = [zz * nx for zz in range(nz)]
    for xx in range(1, nx):
        path += [zz * nx + xx for zz in (range(nz) if xx % 2 == 0 else reversed(range(nz)))]
    place = {dd: i for i, dd in enumerate(path)}

    part = rows // ROW_PARTS
    gathered = []
    for h in range(ROW_PARTS):
        piece = gradient[h * part : (h + 1) * part]
        piece = permute(piece, lambda bb, zz, xx: (bb, zz ^ spread(bb), xx))
        piece = permute(piece, lambda bb, zz, xx: (zz ^ spread(bb), zz, xx))
        gathered.append(lax.all_gather(piece, "dp", axis_index_groups=[path]))

    blocks = lax.all_gather(left_basis.astype(low).T, "dp", axis_index_groups=[path])
    left_t = jnp.concatenate([blocks[place[dd]] for dd in range(nd)], axis=0)
    for i, t in enumerate(reversed(bits)):
        left_t = joined(left_t, move_b(left_t, t), (b & t) != 0, 1 + i)
    left_t = left_t.reshape(whole, whole)
    left = left_t.T

    right = right_basis.astype(low)
    half = jnp.zeros((whole, ff_block), low)
    sources = jnp.array(unspread, jnp.int32)
    for h in range(ROW_PARTS):
        for zz in range(nz):
            total = 0.0
            for xx in range(nx):
                total = total + matmul(
                    gathered[h][place[zz * nx + xx]], right[xx * ff_block : (xx + 1) * ff_block]
                )
            start = sources[b ^ zz] * rows + h * part
            half = lax.dynamic_update_slice_in_dim(half, total.astype(low), start, 0)

    def left_t_rows(t):
        return lax.dynamic_slice_in_dim(left_t, (b ^ t) * rows, rows, 0)

    width = ff_block // COL_PARTS
    first_out, second_out, columns = [], [], []
    for j in range(COL_PARTS):
        cols = slice(j * width, (j + 1) * width)
        part_half = half[:, cols]
        gone = jnp.concatenate([matmul(left_t_rows(t), part_half).astype(low) for t in range(1, nb, 2)], axis=0)
        got = move_b(gone, 1)
        held = {}
        for i, t in enumerate(range(0, nb, 2)):
            held[t] = matmul(left_t_rows(t), part_half) + got[i * rows : (i + 1) * rows].astype(jnp.float32)
        for t in reversed(bits[1:]):
            away = [s for s in held if s & t]
            got = move_b(jnp.concatenate([held[s].astype(low) for s in away], axis=0), t)
            for i, s in enumerate(away):
                held[s ^ t] = held[s ^ t] + got[i * rows : (i + 1) * rows].astype(jnp.float32)
                del held[s]
        rotated = held[0]
        first_new = beta_first * first_moment[:, cols] + (1.0 - beta_first) * rotated
        second_new = beta_second * second_moment[:, cols] + (1.0 - beta_second) * rotated * rotated
        first_fix = 1.0 - beta_first**STEP
        second_fix = 1.0 - beta_second**STEP
        direction = first_new / first_fix / (jnp.sqrt(second_new / second_fix) + epsilon)
        first_out.append(first_new)
        second_out.append(second_new)
        column = direction.astype(low)
        axis = 0
        for t in reversed(bits):
            column = joined(column, move_b(column, t), (b & t) != 0, axis)
            axis += 1
        columns.append(column.reshape(whole, width))
    columns = lax.optimization_barrier(jnp.concatenate(columns, axis=1))

    update = []
    part = out_rows // OUT_PARTS
    for i in range(OUT_PARTS):
        rows_of = jnp.concatenate([left[dd * out_rows + i * part : dd * out_rows + (i + 1) * part] for dd in path], axis=0)
        rows_of = lax.optimization_barrier(rows_of)
        back = matmul(rows_of, columns).astype(low)
        total = matmul_nt(back, right).astype(low)
        update.append(lax.psum_scatter(total, "dp", scatter_dimension=0, axis_index_groups=[path], tiled=True))
    return (
        jnp.concatenate(first_out, axis=1),
        jnp.concatenate(second_out, axis=1),
        jnp.concatenate(update, axis=0),
    )


def solution(mesh):
    nb, nd = mesh.shape["basis"], mesh.shape["dp"]

    def run(*args):
        return per_device(*args, nb=nb, nd=nd)

    return jax.shard_map(
        run,
        mesh=mesh,
        in_specs=(
            P("basis", "dp"),
            P("basis", "dp"),
            P("basis", "dp"),
            P("basis", "dp"),
            P("basis", "dp"),
        ),
        out_specs=(P("basis", "dp"), P("basis", "dp"), P("dp", "basis")),
        check_vma=False,
    )
```

```python
import jax
import jax.numpy as jnp
from jax import lax
from jax.sharding import PartitionSpec as P

STEP = 4


beta_first = 0.95
beta_second = 0.95
epsilon = 1e-08

COL_PARTS = 2

low = jnp.bfloat16


def matmul(a, b):
    return lax.dot_general(a, b, (((1,), (0,)), ((), ())), preferred_element_type=jnp.float32)


def matmul_nt(a, b):
    return lax.dot_general(a, b, (((1,), (1,)), ((), ())), preferred_element_type=jnp.float32)


def per_device(gradient, left_basis, right_basis, first_moment, second_moment, *, nb, nd):
    nz = nb
    nx = nd // nz
    b = lax.axis_index("basis")
    d = lax.axis_index("dp")
    z, x = d // nx, d % nx
    bits = [1 << k for k in range(nb.bit_length() - 1)]
    x_bits = [1 << k for k in range(nx.bit_length() - 1)]

    def permute(value, target):
        pairs = []
        for bb in range(nb):
            for zz in range(nz):
                for xx in range(nx):
                    tb, tz, tx = target(bb, zz, xx)
                    pairs.append((bb * nd + zz * nx + xx, tb * nd + tz * nx + tx))
        return lax.ppermute(value, ("basis", "dp"), pairs)

    def move_b(value, t):
        return permute(value, lambda bb, zz, xx: (bb ^ t, zz, xx))

    def move_z(value, t):
        return permute(value, lambda bb, zz, xx: (bb, zz ^ t, xx))

    def move_x(value, u):
        return permute(value, lambda bb, zz, xx: (bb, zz, xx ^ u))

    def spread(beta):
        return (beta >> 1) ^ ((beta & 1) * (nz - 1))

    unspread = [0] * nz
    for beta in range(nb):
        unspread[spread(beta)] = beta

    def joined(mine, other, bit_set, axis):
        first = jnp.where(bit_set, other, mine)
        second = jnp.where(bit_set, mine, other)
        return jnp.stack([first, second], axis=axis)

    ff_block = right_basis.shape[1]
    rows = first_moment.shape[0]
    out_rows = left_basis.shape[1]
    whole = rows * nb

    path = [zz * nx for zz in range(nz)]
    for xx in range(1, nx):
        path += [zz * nx + xx for zz in (range(nz) if xx % 2 == 0 else reversed(range(nz)))]
    place = {dd: i for i, dd in enumerate(path)}

    def after(value, *others):
        return lax.optimization_barrier((value,) + others)[0]

    left_t = left_basis.astype(low).T
    piece = permute(gradient, lambda bb, zz, xx: (bb, zz ^ spread(bb), xx))
    for i, t in enumerate(reversed(bits[1:])):
        left_t = joined(left_t, move_z(left_t, t), (z & t) != 0, i)
    piece, left_t = lax.optimization_barrier((piece, left_t))
    piece = permute(piece, lambda bb, zz, xx: (zz ^ spread(bb), zz, xx))
    gathered = lax.all_gather(piece, "dp", axis_index_groups=[path])
    for i, u in enumerate(reversed(x_bits)):
        left_t = joined(left_t, move_x(left_t, u), (x & u) != 0, len(bits) - 1 + i)
    left_t = joined(left_t, move_z(left_t, bits[0]), (z & bits[0]) != 0, len(bits) - 1).reshape(whole, rows)
    for t in reversed(bits):
        left_t = jnp.concatenate([left_t, move_b(left_t, t)], axis=1)
    order = [0]
    for t in reversed(bits):
        order = order + [s | t for s in order]
    left_t, gathered = lax.optimization_barrier((left_t, gathered))

    right = right_basis.astype(low)
    half = jnp.zeros((whole, ff_block), low)
    sources = jnp.array(unspread, jnp.int32)
    places = jnp.array([order.index(t) for t in range(nb)], jnp.int32)
    for zz in range(nz):
        total = 0.0
        for xx in range(nx):
            total = total + matmul(gathered[place[zz * nx + xx]], right[xx * ff_block : (xx + 1) * ff_block])
        start = places[sources[b ^ zz] ^ b] * rows
        half = lax.dynamic_update_slice_in_dim(half, total.astype(low), start, 0)

    left = jnp.concatenate(
        [
            lax.dynamic_slice_in_dim(left_t, places[b ^ (dd // nx)] * rows + dd % nx * out_rows, out_rows, 1).T
            for dd in path
        ],
        axis=0,
    )
    left = lax.optimization_barrier(left)

    def left_t_rows(t):
        return lax.dynamic_slice_in_dim(left_t, (b ^ t) * rows, rows, 0)

    width = ff_block // COL_PARTS
    first_out, second_out, columns = [], [], []
    for j in range(COL_PARTS):
        cols = slice(j * width, (j + 1) * width)
        part_half = half[:, cols]
        if j:
            part_half = after(part_half, gone)
        gone = jnp.concatenate([matmul(left_t_rows(t), part_half).astype(low) for t in range(1, nb, 2)], axis=0)
        got = move_b(gone, 1)
        held = {}
        for i, t in enumerate(range(0, nb, 2)):
            held[t] = matmul(left_t_rows(t), part_half) + got[i * rows : (i + 1) * rows].astype(jnp.float32)
        for t in reversed(bits[1:]):
            away = [s for s in held if s & t]
            got = move_b(jnp.concatenate([held[s].astype(low) for s in away], axis=0), t)
            for i, s in enumerate(away):
                held[s ^ t] = held[s ^ t] + got[i * rows : (i + 1) * rows].astype(jnp.float32)
                del held[s]
        rotated = held[0]
        moments = first_moment[:, cols], second_moment[:, cols]
        if j:
            moments = after(moments, previous)
        first_new = beta_first * moments[0] + (1.0 - beta_first) * rotated
        second_new = beta_second * moments[1] + (1.0 - beta_second) * rotated * rotated
        first_fix = 1.0 - beta_first**STEP
        second_fix = 1.0 - beta_second**STEP
        direction = first_new / first_fix / (jnp.sqrt(second_new / second_fix) + epsilon)
        first_out.append(first_new)
        second_out.append(second_new)
        column = previous = direction.astype(low)
        axis = 0
        for t in reversed(bits):
            column = joined(column, move_b(column, t), (b & t) != 0, axis)
            axis += 1
        columns.append(column.reshape(whole, width))
    columns = lax.optimization_barrier(jnp.concatenate(columns, axis=1))

    back = lax.optimization_barrier(matmul(left, columns).astype(low))
    total = matmul_nt(back, right).astype(low)
    update = lax.psum_scatter(total, "dp", scatter_dimension=0, axis_index_groups=[path], tiled=True)
    return (
        jnp.concatenate(first_out, axis=1),
        jnp.concatenate(second_out, axis=1),
        update,
    )


def solution(mesh):
    nb, nd = mesh.shape["basis"], mesh.shape["dp"]

    def run(*args):
        return per_device(*args, nb=nb, nd=nd)

    return jax.shard_map(
        run,
        mesh=mesh,
        in_specs=(
            P("basis", "dp"),
            P("basis", "dp"),
            P("basis", "dp"),
            P("basis", "dp"),
            P("basis", "dp"),
        ),
        out_specs=(P("basis", "dp"), P("basis", "dp"), P("dp", "basis")),
        check_vma=False,
    )
```

```python
import functools

import jax
import jax.numpy as jnp
from jax import lax
from jax.experimental import pallas as pl
from jax.experimental.pallas import tpu as pltpu
from jax.sharding import PartitionSpec as P

STEP = 4


beta_first = 0.95
beta_second = 0.95
epsilon = 1e-08

COL_PARTS = 2

VMEM_BYTES = 48 * 1024 * 1024

low = jnp.bfloat16


def matmul(a, b):
    return lax.dot_general(a, b, (((1,), (0,)), ((), ())), preferred_element_type=jnp.float32)


def matmul_tn(a, b):
    return lax.dot_general(a, b, (((0,), (0,)), ((), ())), preferred_element_type=jnp.float32)


def matmul_nt(a, b):
    return lax.dot_general(a, b, (((1,), (1,)), ((), ())), preferred_element_type=jnp.float32)


def cost(flops, *arrays):
    size = sum(a.size * a.dtype.itemsize for a in arrays)
    return pl.CostEstimate(flops=flops, bytes_accessed=size, transcendentals=0)


def half_rotation(gathered, right, places, nz, parts):
    count, rows, cols = gathered.shape
    nx = count // nz
    width = right.shape[1] // parts

    def kernel(places_ref, *refs):
        blocks, right_ref, outs = refs[:nx], refs[nx], refs[nx + 1 :]
        for j, out in enumerate(outs):
            total = matmul(blocks[0][...], right_ref[:cols, j * width : (j + 1) * width])
            for i in range(1, nx):
                total += matmul(blocks[i][...], right_ref[i * cols : (i + 1) * cols, j * width : (j + 1) * width])
            out[...] = total.astype(out.dtype)

    def block_of(i):
        if i % 2 == 0:
            return pl.BlockSpec((None, rows, cols), lambda k, p: (i * nz + k, 0, 0))
        return pl.BlockSpec((None, rows, cols), lambda k, p: (i * nz + nz - 1 - k, 0, 0))

    outs = [jax.ShapeDtypeStruct((nz * rows, width), low)] * parts
    return pl.pallas_call(
        kernel,
        out_shape=outs,
        grid_spec=pltpu.PrefetchScalarGridSpec(
            num_scalar_prefetch=1,
            grid=(nz,),
            in_specs=[block_of(i) for i in range(nx)]
            + [pl.BlockSpec(right.shape, lambda k, p: (0, 0), pipeline_mode=pl.Buffered(1))],
            out_specs=[pl.BlockSpec((rows, width), lambda k, p: (p[k], 0))] * parts,
        ),
        compiler_params=pltpu.CompilerParams(vmem_limit_bytes=VMEM_BYTES),
        cost_estimate=cost(2 * gathered.size * right.shape[1], gathered, right, *outs),
        name="half_rotation",
    )(places, *([gathered] * nx), right)


def back_rotation(columns, right, places, block):
    parts = len(columns)
    total_rows, width = columns[0].shape
    count = total_rows // block

    def kernel(places_ref, *refs):
        rows_of, right_ref, out = refs[:parts], refs[parts], refs[parts + 1]
        total = matmul_nt(rows_of[0][...], right_ref[:, :width])
        for j in range(1, parts):
            total += matmul_nt(rows_of[j][...], right_ref[:, j * width : (j + 1) * width])
        out[...] = total.astype(out.dtype)

    out = jax.ShapeDtypeStruct((total_rows, right.shape[0]), low)
    return pl.pallas_call(
        kernel,
        out_shape=out,
        grid_spec=pltpu.PrefetchScalarGridSpec(
            num_scalar_prefetch=1,
            grid=(count,),
            in_specs=[pl.BlockSpec((block, width), lambda k, p: (p[k], 0))] * parts
            + [pl.BlockSpec(right.shape, lambda k, p: (0, 0), pipeline_mode=pl.Buffered(1))],
            out_specs=pl.BlockSpec((block, right.shape[0]), lambda k, p: (k, 0)),
        ),
        compiler_params=pltpu.CompilerParams(vmem_limit_bytes=VMEM_BYTES),
        cost_estimate=cost(2 * total_rows * right.size, right, out, *columns),
        name="back_rotation",
    )(places, *columns, right)


def per_device(gradient, left_basis, right_basis, first_moment, second_moment, *, nb, nd):
    nz = nb
    nx = nd // nz
    b = lax.axis_index("basis")
    d = lax.axis_index("dp")
    z, x = d // nx, d % nx
    bits = [1 << k for k in range(nb.bit_length() - 1)]
    x_bits = [1 << k for k in range(nx.bit_length() - 1)]

    def permute(value, target):
        pairs = []
        for bb in range(nb):
            for zz in range(nz):
                for xx in range(nx):
                    tb, tz, tx = target(bb, zz, xx)
                    pairs.append((bb * nd + zz * nx + xx, tb * nd + tz * nx + tx))
        return lax.ppermute(value, ("basis", "dp"), pairs)

    def move_b(value, t):
        return permute(value, lambda bb, zz, xx: (bb ^ t, zz, xx))

    def move_z(value, t):
        return permute(value, lambda bb, zz, xx: (bb, zz ^ t, xx))

    def move_x(value, u):
        return permute(value, lambda bb, zz, xx: (bb, zz, xx ^ u))

    def spread(beta):
        return (beta >> 1) ^ ((beta & 1) * (nz - 1))

    unspread = [0] * nz
    for beta in range(nb):
        unspread[spread(beta)] = beta

    def joined(mine, other, bit_set, axis):
        first = jnp.where(bit_set, other, mine)
        second = jnp.where(bit_set, mine, other)
        return jnp.stack([first, second], axis=axis)

    def after(value, *others):
        return lax.optimization_barrier((value,) + others)[0]

    ff_block = right_basis.shape[1]
    rows = first_moment.shape[0]
    out_rows = left_basis.shape[1]
    whole = rows * nb

    path = []
    for xx in range(nx):
        path += [zz * nx + xx for zz in (range(nz) if xx % 2 == 0 else reversed(range(nz)))]

    order = [0]
    for t in reversed(bits):
        order = order + [s | t for s in order]
    half_places = [[order.index(unspread[bb ^ zz] ^ bb) for zz in range(nz)] for bb in range(nb)]
    back_places = [[order.index(bb ^ (dd // nx)) * nx + dd % nx for dd in path] for bb in range(nb)]
    half_places = jnp.array(half_places, jnp.int32)[b]
    back_places = jnp.array(back_places, jnp.int32)[b]

    left_t = left_basis.astype(low).T
    right = right_basis.astype(low)
    piece = permute(gradient, lambda bb, zz, xx: (bb, zz ^ spread(bb), xx))
    for i, u in enumerate(reversed(x_bits)):
        left_t = joined(left_t, move_x(left_t, u), (x & u) != 0, i)
    for i, t in enumerate(reversed(bits[1:])):
        left_t = joined(left_t, move_z(left_t, t), (z & t) != 0, i)
    piece, left_t, right, half_places, back_places = lax.optimization_barrier(
        (piece, left_t, right, half_places, back_places)
    )
    piece = permute(piece, lambda bb, zz, xx: (zz ^ spread(bb), zz, xx))
    gathered = lax.all_gather(piece, "dp", axis_index_groups=[path])
    left_t = joined(left_t, move_z(left_t, bits[0]), (z & bits[0]) != 0, len(bits) - 1).reshape(whole, rows)
    for t in reversed(bits):
        left_t = jnp.concatenate([left_t, move_b(left_t, t)], axis=1)
    left_t, gathered = lax.optimization_barrier((left_t, gathered))

    half = list(half_rotation(gathered, right, half_places, nz, COL_PARTS))

    def product(t, j):
        rows_of = lax.dynamic_slice_in_dim(left_t, (b ^ t) * rows, rows, 0)
        return matmul(rows_of, half[j]).astype(low)

    width = ff_block // COL_PARTS
    first_out, second_out, back = [], [], []
    for j in range(COL_PARTS):
        cols = slice(j * width, (j + 1) * width)
        if j:
            half[j] = after(half[j], gone)
        gone = lax.optimization_barrier([product(t, j) for t in range(1, nb, 2)])
        gots = [move_b(value, 1) for value in gone]
        held = dict(zip(range(0, nb, 2), lax.optimization_barrier([product(t, j) for t in range(0, nb, 2)])))
        held = {t: held[t].astype(jnp.float32) + got.astype(jnp.float32) for t, got in zip(held, gots)}
        for t in reversed(bits[1:]):
            for s in [s for s in held if s & t]:
                held[s ^ t] = held[s ^ t] + move_b(held.pop(s).astype(low), t).astype(jnp.float32)
        rotated = held[0]
        moments = first_moment[:, cols], second_moment[:, cols]
        if j:
            moments = after(moments, previous)
        first_new = beta_first * moments[0] + (1.0 - beta_first) * rotated
        second_new = beta_second * moments[1] + (1.0 - beta_second) * rotated * rotated
        first_fix = 1.0 - beta_first**STEP
        second_fix = 1.0 - beta_second**STEP
        direction = first_new / first_fix / (jnp.sqrt(second_new / second_fix) + epsilon)
        first_out.append(first_new)
        second_out.append(second_new)
        column = previous = direction.astype(low)
        axis = 0
        for t in reversed(bits):
            column = joined(column, move_b(column, t), (b & t) != 0, axis)
            axis += 1
        column = lax.optimization_barrier(column.reshape(whole, width))
        back.append(lax.optimization_barrier(matmul_tn(left_t, column).astype(low)))

    total = back_rotation(back, right, back_places, out_rows)
    update = lax.psum_scatter(total, "dp", scatter_dimension=0, axis_index_groups=[path], tiled=True)
    return (
        jnp.concatenate(first_out, axis=1),
        jnp.concatenate(second_out, axis=1),
        update,
    )


def solution(mesh):
    nb, nd = mesh.shape["basis"], mesh.shape["dp"]

    return jax.shard_map(
        functools.partial(per_device, nb=nb, nd=nd),
        mesh=mesh,
        in_specs=(
            P("basis", "dp"),
            P("basis", "dp"),
            P("basis", "dp"),
            P("basis", "dp"),
            P("basis", "dp"),
        ),
        out_specs=(P("basis", "dp"), P("basis", "dp"), P("dp", "basis")),
        check_vma=False,
    )
```

```python
import functools

import jax
import jax.numpy as jnp
from jax import lax
from jax.experimental import pallas as pl
from jax.experimental.pallas import tpu as pltpu
from jax.sharding import PartitionSpec as P

STEP = 4


beta_first = 0.95
beta_second = 0.95
epsilon = 1e-08

COL_PARTS = 2

VMEM_BYTES = 48 * 1024 * 1024

low = jnp.bfloat16


def matmul(a, b):
    return lax.dot_general(a, b, (((1,), (0,)), ((), ())), preferred_element_type=jnp.float32)


def cost(flops, *arrays):
    size = sum(a.size * a.dtype.itemsize for a in arrays)
    return pl.CostEstimate(flops=flops, bytes_accessed=size, transcendentals=0)


def half_rotation(gathered, right, places, nz, parts):
    count, rows, cols = gathered.shape
    nx = count // nz
    width = right.shape[1] // parts

    def kernel(places_ref, *refs):
        blocks, right_ref, outs = refs[:nx], refs[nx], refs[nx + 1 :]
        for j, out in enumerate(outs):
            total = matmul(blocks[0][...], right_ref[:cols, j * width : (j + 1) * width])
            for i in range(1, nx):
                total += matmul(blocks[i][...], right_ref[i * cols : (i + 1) * cols, j * width : (j + 1) * width])
            out[...] = total.astype(out.dtype)

    def block_of(i):
        if i % 2 == 0:
            return pl.BlockSpec((None, rows, cols), lambda k, p: (i * nz + k, 0, 0))
        return pl.BlockSpec((None, rows, cols), lambda k, p: (i * nz + nz - 1 - k, 0, 0))

    outs = [jax.ShapeDtypeStruct((nz * rows, width), low)] * parts
    return pl.pallas_call(
        kernel,
        out_shape=outs,
        grid_spec=pltpu.PrefetchScalarGridSpec(
            num_scalar_prefetch=1,
            grid=(nz,),
            in_specs=[block_of(i) for i in range(nx)]
            + [pl.BlockSpec(right.shape, lambda k, p: (0, 0), pipeline_mode=pl.Buffered(1))],
            out_specs=[pl.BlockSpec((rows, width), lambda k, p: (p[k], 0))] * parts,
        ),
        compiler_params=pltpu.CompilerParams(vmem_limit_bytes=VMEM_BYTES),
        cost_estimate=cost(2 * gathered.size * right.shape[1], gathered, right, *outs),
        name="half_rotation",
    )(places, *([gathered] * nx), right)


def back_rotation(columns, right_t, block):
    parts = len(columns)
    total_rows, width = columns[0].shape

    def kernel(*refs):
        rows_of, right_ref, out = refs[:parts], refs[parts], refs[parts + 1]
        total = matmul(rows_of[0][...], right_ref[:width])
        for j in range(1, parts):
            total += matmul(rows_of[j][...], right_ref[j * width : (j + 1) * width])
        out[...] = total.astype(out.dtype)

    out = jax.ShapeDtypeStruct((total_rows, right_t.shape[1]), low)
    return pl.pallas_call(
        kernel,
        out_shape=out,
        grid=(total_rows // block,),
        in_specs=[pl.BlockSpec((block, width), lambda k: (k, 0))] * parts
        + [pl.BlockSpec(right_t.shape, lambda k: (0, 0), pipeline_mode=pl.Buffered(1))],
        out_specs=pl.BlockSpec((block, right_t.shape[1]), lambda k: (k, 0)),
        compiler_params=pltpu.CompilerParams(vmem_limit_bytes=VMEM_BYTES),
        cost_estimate=cost(2 * total_rows * right_t.size, right_t, out, *columns),
        name="back_rotation",
    )(*columns, right_t)


def per_device(gradient, left_basis, right_basis, first_moment, second_moment, *, nb, nd):
    nz = nb
    nx = nd // nz
    b = lax.axis_index("basis")
    d = lax.axis_index("dp")
    z, x = d // nx, d % nx
    bits = [1 << k for k in range(nb.bit_length() - 1)]
    x_bits = [1 << k for k in range(nx.bit_length() - 1)]

    def permute(value, target):
        pairs = []
        for bb in range(nb):
            for zz in range(nz):
                for xx in range(nx):
                    tb, tz, tx = target(bb, zz, xx)
                    pairs.append((bb * nd + zz * nx + xx, tb * nd + tz * nx + tx))
        return lax.ppermute(value, ("basis", "dp"), pairs)

    def move_b(value, t):
        return permute(value, lambda bb, zz, xx: (bb ^ t, zz, xx))

    def move_z(value, t):
        return permute(value, lambda bb, zz, xx: (bb, zz ^ t, xx))

    def move_x(value, u):
        return permute(value, lambda bb, zz, xx: (bb, zz, xx ^ u))

    def spread(beta):
        return (beta >> 1) ^ ((beta & 1) * (nz - 1))

    unspread = [0] * nz
    for beta in range(nb):
        unspread[spread(beta)] = beta

    def joined(mine, other, bit_set, axis):
        first = jnp.where(bit_set, other, mine)
        second = jnp.where(bit_set, mine, other)
        return jnp.stack([first, second], axis=axis)

    def after(value, *others):
        return lax.optimization_barrier((value,) + others)[0]

    ff_block = right_basis.shape[1]
    rows = first_moment.shape[0]
    out_rows = left_basis.shape[1]
    whole = rows * nb

    path = []
    for xx in range(nx):
        path += [zz * nx + xx for zz in (range(nz) if xx % 2 == 0 else reversed(range(nz)))]

    order = [0]
    for t in reversed(bits):
        order = order + [s | t for s in order]
    half_places = [[order.index(unspread[bb ^ zz] ^ bb) for zz in range(nz)] for bb in range(nb)]
    half_places = jnp.array(half_places, jnp.int32)[b]
    order_of = jnp.array([order.index(t) for t in range(nb)], jnp.int32)
    path_places = [order_of[b ^ (dd // nx)] * rows + dd % nx * out_rows for dd in path]

    left_t = left_basis.astype(low).T
    right = right_basis.astype(low)
    right_t = right.T
    piece = permute(gradient, lambda bb, zz, xx: (bb, zz ^ spread(bb), xx))
    for i, t in enumerate(reversed(bits)):
        left_t = joined(left_t, move_z(left_t, t), (z & t) != 0, i)
    piece, left_t, right, right_t, half_places, path_places = lax.optimization_barrier(
        (piece, left_t, right, right_t, half_places, path_places)
    )
    piece = permute(piece, lambda bb, zz, xx: (zz ^ spread(bb), zz, xx))
    gathered = lax.all_gather(piece, "dp", axis_index_groups=[path])
    for i, u in enumerate(reversed(x_bits)):
        other, piece = lax.optimization_barrier((move_x(left_t, u), piece))
        left_t = joined(left_t, other, (x & u) != 0, len(bits) + i)
    left_t = left_t.reshape(whole, rows)
    for t in reversed(bits):
        left_t = jnp.concatenate([left_t, move_b(left_t, t)], axis=1)
    left_t = lax.optimization_barrier(left_t)
    left = jnp.concatenate(
        [lax.dynamic_slice_in_dim(left_t, start, out_rows, 1).T for start in path_places], axis=0
    )
    left_t, left, gathered = lax.optimization_barrier((left_t, left, gathered))

    half = list(half_rotation(gathered, right, half_places, nz, COL_PARTS))

    def product(t, j):
        rows_of = lax.dynamic_slice_in_dim(left_t, (b ^ t) * rows, rows, 0)
        return matmul(rows_of, half[j]).astype(low)

    width = ff_block // COL_PARTS
    first_out, second_out, back, joins = [], [], [], []
    for j in range(COL_PARTS):
        cols = slice(j * width, (j + 1) * width)
        if j:
            half[j] = after(half[j], gone)
        gone = lax.optimization_barrier([product(t, j) for t in range(1, nb, 2)])
        gots = [move_b(value, 1) for value in gone]
        held = dict(zip(range(0, nb, 2), lax.optimization_barrier([product(t, j) for t in range(0, nb, 2)])))
        held = {t: held[t].astype(jnp.float32) + got.astype(jnp.float32) for t, got in zip(held, gots)}
        for t in reversed(bits[1:]):
            for s in [s for s in held if s & t]:
                away = held.pop(s).astype(low)
                if j:
                    away = after(away, summed)
                held[s ^ t] = held[s ^ t] + move_b(away, t).astype(jnp.float32)
        rotated = summed = held[0]
        moments = first_moment[:, cols], second_moment[:, cols]
        if j:
            moments = after(moments, previous)
        first_new = beta_first * moments[0] + (1.0 - beta_first) * rotated
        second_new = beta_second * moments[1] + (1.0 - beta_second) * rotated * rotated
        first_fix = 1.0 - beta_first**STEP
        second_fix = 1.0 - beta_second**STEP
        direction = first_new / first_fix / (jnp.sqrt(second_new / second_fix) + epsilon)
        first_out.append(first_new)
        second_out.append(second_new)
        column = previous = direction.astype(low)
        axis = 0
        for t in reversed(bits):
            other = move_b(column, t)
            if j:
                other = after(other, joins[axis])
            column = joined(column, other, (b & t) != 0, axis)
            joins[axis : axis + 1] = [column]
            axis += 1
        column = lax.optimization_barrier(column.reshape(whole, width))
        back.append(lax.optimization_barrier(matmul(left, column).astype(low)))

    total = back_rotation(back, right_t, rows)
    update = lax.psum_scatter(total, "dp", scatter_dimension=0, axis_index_groups=[path], tiled=True)
    return (
        jnp.concatenate(first_out, axis=1),
        jnp.concatenate(second_out, axis=1),
        update,
    )


def solution(mesh):
    nb, nd = mesh.shape["basis"], mesh.shape["dp"]

    return jax.shard_map(
        functools.partial(per_device, nb=nb, nd=nd),
        mesh=mesh,
        in_specs=(
            P("basis", "dp"),
            P("basis", "dp"),
            P("basis", "dp"),
            P("basis", "dp"),
            P("basis", "dp"),
        ),
        out_specs=(P("basis", "dp"), P("basis", "dp"), P("dp", "basis")),
        check_vma=False,
    )
```

```python
import functools

import jax
import jax.numpy as jnp
from jax import lax
from jax.experimental import pallas as pl
from jax.experimental.pallas import tpu as pltpu
from jax.sharding import PartitionSpec as P

STEP = 4


beta_first = 0.95
beta_second = 0.95
epsilon = 1e-08

ROW_PARTS = 2
COL_PARTS = 2

VMEM_BYTES = 48 * 1024 * 1024

low = jnp.bfloat16


def matmul(a, b):
    return lax.dot_general(a, b, (((1,), (0,)), ((), ())), preferred_element_type=jnp.float32)


def matmul_nt(a, b):
    return lax.dot_general(a, b, (((1,), (1,)), ((), ())), preferred_element_type=jnp.float32)


def cost(flops, *arrays):
    size = sum(a.size * a.dtype.itemsize for a in arrays)
    return pl.CostEstimate(flops=flops, bytes_accessed=size, transcendentals=0)


def half_rotation(gathered, right, places, nz, parts, part, row_parts, held):
    count, rows, cols = gathered.shape
    nx = count // nz
    width = right.shape[1] // parts

    def kernel(places_ref, *refs):
        blocks, right_ref, outs = refs[:nx], refs[nx], refs[-parts:]
        for j, out in enumerate(outs):
            total = matmul(blocks[0][...], right_ref[:cols, j * width : (j + 1) * width])
            for i in range(1, nx):
                total += matmul(blocks[i][...], right_ref[i * cols : (i + 1) * cols, j * width : (j + 1) * width])
            out[...] = total.astype(out.dtype)

    def block_of(i):
        if i % 2 == 0:
            return pl.BlockSpec((None, rows, cols), lambda k, p: (i * nz + k, 0, 0))
        return pl.BlockSpec((None, rows, cols), lambda k, p: (i * nz + nz - 1 - k, 0, 0))

    outs = [jax.ShapeDtypeStruct((nz * rows * row_parts, width), low)] * parts
    return pl.pallas_call(
        kernel,
        out_shape=outs,
        grid_spec=pltpu.PrefetchScalarGridSpec(
            num_scalar_prefetch=1,
            grid=(nz,),
            in_specs=[block_of(i) for i in range(nx)]
            + [pl.BlockSpec(right.shape, lambda k, p: (0, 0), pipeline_mode=pl.Buffered(1))]
            + [pl.BlockSpec(memory_space=pl.ANY)] * len(held),
            out_specs=[pl.BlockSpec((rows, width), lambda k, p: (p[k] * row_parts + part, 0))] * parts,
        ),
        input_output_aliases={nx + 2 + j: j for j in range(len(held))},
        compiler_params=pltpu.CompilerParams(vmem_limit_bytes=VMEM_BYTES),
        cost_estimate=cost(2 * gathered.size * right.shape[1], gathered, right, *outs),
        name="half_rotation",
    )(places, *([gathered] * nx), right, *held)


def per_device(gradient, left_basis, right_basis, first_moment, second_moment, *, nb, nd):
    nz = nb
    nx = nd // nz
    b = lax.axis_index("basis")
    d = lax.axis_index("dp")
    z, x = d // nx, d % nx
    bits = [1 << k for k in range(nb.bit_length() - 1)]
    x_bits = [1 << k for k in range(nx.bit_length() - 1)]

    def permute(value, target):
        pairs = []
        for bb in range(nb):
            for zz in range(nz):
                for xx in range(nx):
                    tb, tz, tx = target(bb, zz, xx)
                    pairs.append((bb * nd + zz * nx + xx, tb * nd + tz * nx + tx))
        return lax.ppermute(value, ("basis", "dp"), pairs)

    def move_b(value, t):
        return permute(value, lambda bb, zz, xx: (bb ^ t, zz, xx))

    def move_z(value, t):
        return permute(value, lambda bb, zz, xx: (bb, zz ^ t, xx))

    def move_x(value, u):
        return permute(value, lambda bb, zz, xx: (bb, zz, xx ^ u))

    def spread(beta):
        return (beta >> 1) ^ ((beta & 1) * (nz - 1))

    unspread = [0] * nz
    for beta in range(nb):
        unspread[spread(beta)] = beta

    def joined(mine, other, bit_set, axis):
        first = jnp.where(bit_set, other, mine)
        second = jnp.where(bit_set, mine, other)
        return jnp.stack([first, second], axis=axis)

    def after(value, *others):
        return lax.optimization_barrier((value,) + others)[0]

    ff_block = right_basis.shape[1]
    rows = first_moment.shape[0]
    out_rows = left_basis.shape[1]
    whole = rows * nb

    path = []
    for xx in range(nx):
        path += [zz * nx + xx for zz in (range(nz) if xx % 2 == 0 else reversed(range(nz)))]

    order = [0]
    for t in reversed(bits):
        order = order + [s | t for s in order]
    half_places = [[order.index(unspread[bb ^ zz] ^ bb) for zz in range(nz)] for bb in range(nb)]
    half_places = jnp.array(half_places, jnp.int32)[b]
    order_of = jnp.array([order.index(t) for t in range(nb)], jnp.int32)
    path_places = [order_of[b ^ (dd // nx)] * rows + dd % nx * out_rows for dd in path]

    def together(*values):
        return lax.optimization_barrier(values)

    left_t = left_basis.astype(low).T
    right = right_basis.astype(low)
    part = rows // ROW_PARTS
    pieces = [gradient[h * part : (h + 1) * part] for h in range(ROW_PARTS)]

    def across(piece):
        return permute(piece, lambda bb, zz, xx: (bb, zz ^ spread(bb), xx))

    def along(piece):
        return permute(piece, lambda bb, zz, xx: (zz ^ spread(bb), zz, xx))

    def gather(piece):
        return lax.all_gather(piece, "dp", axis_index_groups=[path])

    def left_steps():
        value = left_t
        for i, t in enumerate(reversed(bits)):
            value = joined(value, (yield move_z(value, t)), (z & t) != 0, i)
        for i, u in enumerate(reversed(x_bits)):
            value = joined(value, (yield move_x(value, u)), (x & u) != 0, len(bits) + i)
        value = value.reshape(whole, rows)
        for t in reversed(bits):
            value = jnp.concatenate([value, (yield move_b(value, t))], axis=1)
        yield value

    steps = left_steps()
    step = next(steps)
    gathered = []
    pieces[0] = across(pieces[0])
    for h in range(ROW_PARTS):
        pieces[h], step, right, half_places = together(pieces[h], step, right, half_places)
        moved = along(pieces[h])
        if h + 1 < ROW_PARTS:
            pieces[h + 1] = across(after(pieces[h + 1], pieces[h]))
        step = steps.send(step)
        gathered.append(gather(moved))
        if h + 1 < ROW_PARTS:
            pieces[h + 1], step, _ = together(pieces[h + 1], step, moved)
        else:
            step, _ = together(step, moved)
    left_t = step
    while left_t.shape != (whole, whole):
        left_t = steps.send(left_t)
    left_t, gathered[-1] = together(left_t, gathered[-1])
    left = jnp.concatenate(
        [lax.dynamic_slice_in_dim(left_t, start, out_rows, 1).T for start in path_places], axis=0
    )
    left = lax.optimization_barrier(left)

    half = []
    for h in range(ROW_PARTS):
        half = list(half_rotation(gathered[h], right, half_places, nz, COL_PARTS, h, ROW_PARTS, half))

    def product(t, j):
        rows_of = lax.dynamic_slice_in_dim(left_t, (b ^ t) * rows, rows, 0)
        return matmul(rows_of, half[j]).astype(low)

    width = ff_block // COL_PARTS
    first_out, second_out, columns, joins = [], [], [], []
    for j in range(COL_PARTS):
        cols = slice(j * width, (j + 1) * width)
        if j:
            half[j] = after(half[j], gone)
        gone = lax.optimization_barrier([product(t, j) for t in range(1, nb, 2)])
        gots = [move_b(value, 1) for value in gone]
        held = dict(zip(range(0, nb, 2), lax.optimization_barrier([product(t, j) for t in range(0, nb, 2)])))
        held = {t: held[t].astype(jnp.float32) + got.astype(jnp.float32) for t, got in zip(held, gots)}
        for t in reversed(bits[1:]):
            for s in [s for s in held if s & t]:
                away = held.pop(s).astype(low)
                if j:
                    away = after(away, summed)
                arrived = move_b(away, t)
                held[s ^ t] = held[s ^ t] + arrived.astype(jnp.float32)
        rotated, summed = held[0], arrived
        moments = first_moment[:, cols], second_moment[:, cols]
        if j:
            moments = after(moments, previous)
        first_new = beta_first * moments[0] + (1.0 - beta_first) * rotated
        second_new = beta_second * moments[1] + (1.0 - beta_second) * rotated * rotated
        first_fix = 1.0 - beta_first**STEP
        second_fix = 1.0 - beta_second**STEP
        direction = first_new / first_fix / (jnp.sqrt(second_new / second_fix) + epsilon)
        first_out.append(first_new)
        second_out.append(second_new)
        column = previous = direction.astype(low)
        axis = 0
        for t in reversed(bits):
            other = move_b(column, t)
            if j:
                other = after(other, joins[axis])
            column = joined(column, other, (b & t) != 0, axis)
            joins[axis : axis + 1] = [column]
            axis += 1
        columns.append(column.reshape(whole, width))

    columns = lax.optimization_barrier(jnp.concatenate(columns, axis=1))
    back = lax.optimization_barrier(matmul(left, columns).astype(low))
    total = matmul_nt(back, right).astype(low)
    update = lax.psum_scatter(total, "dp", scatter_dimension=0, axis_index_groups=[path], tiled=True)
    return (
        jnp.concatenate(first_out, axis=1),
        jnp.concatenate(second_out, axis=1),
        update,
    )


def solution(mesh):
    nb, nd = mesh.shape["basis"], mesh.shape["dp"]

    return jax.shard_map(
        functools.partial(per_device, nb=nb, nd=nd),
        mesh=mesh,
        in_specs=(
            P("basis", "dp"),
            P("basis", "dp"),
            P("basis", "dp"),
            P("basis", "dp"),
            P("basis", "dp"),
        ),
        out_specs=(P("basis", "dp"), P("basis", "dp"), P("dp", "basis")),
        check_vma=False,
    )
```

```python
import functools

import jax
import jax.numpy as jnp
from jax import lax
from jax.experimental import pallas as pl
from jax.experimental.pallas import tpu as pltpu
from jax.sharding import PartitionSpec as P

STEP = 4


beta_first = 0.95
beta_second = 0.95
epsilon = 1e-08

COL_PARTS = 2

VMEM_BYTES = 20 * 1024 * 1024

low = jnp.bfloat16


def matmul(a, b):
    return lax.dot_general(a, b, (((1,), (0,)), ((), ())), preferred_element_type=jnp.float32)


def matmul_nt(a, b):
    return lax.dot_general(a, b, (((1,), (1,)), ((), ())), preferred_element_type=jnp.float32)


def cost(flops, *arrays):
    size = sum(a.size * a.dtype.itemsize for a in arrays)
    return pl.CostEstimate(flops=flops, bytes_accessed=size, transcendentals=0)


def half_rotation(gathered, right, places, nz, parts):
    count, rows, cols = gathered.shape
    nx = count // nz
    width = right.shape[1] // parts

    def kernel(places_ref, *refs):
        blocks, right_ref, outs = refs[:nx], refs[nx], refs[nx + 1 :]
        for j, out in enumerate(outs):
            total = matmul(blocks[0][...], right_ref[:cols, j * width : (j + 1) * width])
            for i in range(1, nx):
                total += matmul(blocks[i][...], right_ref[i * cols : (i + 1) * cols, j * width : (j + 1) * width])
            out[...] = total.astype(out.dtype)

    def block_of(i):
        if i % 2 == 0:
            return pl.BlockSpec((None, rows, cols), lambda k, p: (i * nz + k, 0, 0))
        return pl.BlockSpec((None, rows, cols), lambda k, p: (i * nz + nz - 1 - k, 0, 0))

    outs = [jax.ShapeDtypeStruct((nz * rows, width), low)] * parts
    return pl.pallas_call(
        kernel,
        out_shape=outs,
        grid_spec=pltpu.PrefetchScalarGridSpec(
            num_scalar_prefetch=1,
            grid=(nz,),
            in_specs=[block_of(i) for i in range(nx)]
            + [pl.BlockSpec(right.shape, lambda k, p: (0, 0), pipeline_mode=pl.Buffered(1))],
            out_specs=[pl.BlockSpec((rows, width), lambda k, p: (p[k], 0))] * parts,
        ),
        compiler_params=pltpu.CompilerParams(vmem_limit_bytes=VMEM_BYTES),
        cost_estimate=cost(2 * gathered.size * right.shape[1], gathered, right, *outs),
        name="half_rotation",
    )(places, *([gathered] * nx), right)


def per_device(gradient, left_basis, right_basis, first_moment, second_moment, *, nb, nd):
    nz = nb
    nx = nd // nz
    b = lax.axis_index("basis")
    d = lax.axis_index("dp")
    z, x = d // nx, d % nx
    bits = [1 << k for k in range(nb.bit_length() - 1)]
    x_bits = [1 << k for k in range(nx.bit_length() - 1)]

    def permute(value, target):
        pairs = []
        for bb in range(nb):
            for zz in range(nz):
                for xx in range(nx):
                    tb, tz, tx = target(bb, zz, xx)
                    pairs.append((bb * nd + zz * nx + xx, tb * nd + tz * nx + tx))
        return lax.ppermute(value, ("basis", "dp"), pairs)

    def move_b(value, t):
        return permute(value, lambda bb, zz, xx: (bb ^ t, zz, xx))

    def move_z(value, t):
        return permute(value, lambda bb, zz, xx: (bb, zz ^ t, xx))

    def move_x(value, u):
        return permute(value, lambda bb, zz, xx: (bb, zz, xx ^ u))

    def spread(beta):
        return (beta >> 1) ^ ((beta & 1) * (nz - 1))

    unspread = [0] * nz
    for beta in range(nb):
        unspread[spread(beta)] = beta

    def joined(mine, other, bit_set, axis):
        first = jnp.where(bit_set, other, mine)
        second = jnp.where(bit_set, mine, other)
        return jnp.stack([first, second], axis=axis)

    def after(value, *others):
        return lax.optimization_barrier((value,) + others)[0]

    ff_block = right_basis.shape[1]
    rows = first_moment.shape[0]
    out_rows = left_basis.shape[1]
    whole = rows * nb

    path = []
    for xx in range(nx):
        path += [zz * nx + xx for zz in (range(nz) if xx % 2 == 0 else reversed(range(nz)))]

    order = [0]
    for t in reversed(bits):
        order = order + [s | t for s in order]
    half_places = [[order.index(unspread[bb ^ zz] ^ bb) for zz in range(nz)] for bb in range(nb)]
    half_places = jnp.array(half_places, jnp.int32)[b]
    order_of = jnp.array([order.index(t) for t in range(nb)], jnp.int32)
    path_places = [order_of[b ^ (dd // nx)] * rows + dd % nx * out_rows for dd in path]

    def together(*values):
        return lax.optimization_barrier(values)

    left_t = left_basis.astype(low).T
    right = right_basis.astype(low)

    def across(piece):
        return permute(piece, lambda bb, zz, xx: (bb, zz ^ spread(bb), xx))

    def along(piece):
        return permute(piece, lambda bb, zz, xx: (zz ^ spread(bb), zz, xx))

    piece = across(gradient)
    for i, t in enumerate(reversed(bits)):
        left_t = joined(left_t, move_z(left_t, t), (z & t) != 0, i)
    piece, left_t, right, half_places = together(piece, left_t, right, half_places)
    piece = along(piece)
    for i, u in enumerate(reversed(x_bits)):
        other, piece = together(move_x(left_t, u), piece)
        left_t = joined(left_t, other, (x & u) != 0, len(bits) + i)
    gathered = lax.all_gather(piece, "dp", axis_index_groups=[path])
    left_t = left_t.reshape(whole, rows)
    for t in reversed(bits):
        left_t = jnp.concatenate([left_t, move_b(left_t, t)], axis=1)
    left_t, gathered = together(left_t, gathered)
    left = jnp.concatenate(
        [lax.dynamic_slice_in_dim(left_t, start, out_rows, 1).T for start in path_places], axis=0
    )
    left = lax.optimization_barrier(left)

    half = half_rotation(gathered, right, half_places, nz, COL_PARTS)

    odd = sorted(range(1, nb, 2), key=lambda t: -t)
    groups = odd[: nb // 4], odd[nb // 4 :]
    turns = [(t ^ f, j) for group in groups for j in range(COL_PARTS) for t in group for f in (0, 1)]
    products = {}
    last = None
    for t, j in turns:
        rows_of = lax.dynamic_slice_in_dim(left_t, (b ^ t) * rows, rows, 0)
        part = half[j] if last is None else after(half[j], last)
        last = products[t, j] = lax.optimization_barrier(matmul(rows_of, part).astype(low))

    width = ff_block // COL_PARTS
    first_out, second_out, columns, joins = [], [], [], []
    for j in range(COL_PARTS):
        cols = slice(j * width, (j + 1) * width)
        held = {}
        for t in odd:
            held[t ^ 1] = products[t ^ 1, j].astype(jnp.float32) + move_b(products[t, j], 1).astype(jnp.float32)
        for t in reversed(bits[1:]):
            for s in [s for s in held if s & t]:
                away = held.pop(s).astype(low)
                if j:
                    away = after(away, summed)
                arrived = move_b(away, t)
                held[s ^ t] = held[s ^ t] + arrived.astype(jnp.float32)
        rotated, summed = held[0], arrived
        moments = first_moment[:, cols], second_moment[:, cols]
        if j:
            moments = after(moments, previous)
        first_new = beta_first * moments[0] + (1.0 - beta_first) * rotated
        second_new = beta_second * moments[1] + (1.0 - beta_second) * rotated * rotated
        first_fix = 1.0 - beta_first**STEP
        second_fix = 1.0 - beta_second**STEP
        direction = first_new / first_fix / (jnp.sqrt(second_new / second_fix) + epsilon)
        first_out.append(first_new)
        second_out.append(second_new)
        column = previous = direction.astype(low)
        axis = 0
        for t in reversed(bits):
            other = move_b(column, t)
            if j:
                other = after(other, joins[axis])
            column = joined(column, other, (b & t) != 0, axis)
            joins[axis : axis + 1] = [column]
            axis += 1
        columns.append(column.reshape(whole, width))

    columns = lax.optimization_barrier(jnp.concatenate(columns, axis=1))
    back = lax.optimization_barrier(matmul(left, columns).astype(low))
    total = matmul_nt(back, right).astype(low)
    update = lax.psum_scatter(total, "dp", scatter_dimension=0, axis_index_groups=[path], tiled=True)
    return (
        jnp.concatenate(first_out, axis=1),
        jnp.concatenate(second_out, axis=1),
        update,
    )


def solution(mesh):
    nb, nd = mesh.shape["basis"], mesh.shape["dp"]

    return jax.shard_map(
        functools.partial(per_device, nb=nb, nd=nd),
        mesh=mesh,
        in_specs=(
            P("basis", "dp"),
            P("basis", "dp"),
            P("basis", "dp"),
            P("basis", "dp"),
            P("basis", "dp"),
        ),
        out_specs=(P("basis", "dp"), P("basis", "dp"), P("dp", "basis")),
        check_vma=False,
    )
```

```python
import functools

import jax
import jax.numpy as jnp
from jax import lax
from jax.experimental import pallas as pl
from jax.experimental.pallas import tpu as pltpu
from jax.sharding import PartitionSpec as P

STEP = 4


beta_first = 0.95
beta_second = 0.95
epsilon = 1e-08

COL_PARTS = 2

VMEM_BYTES = 20 * 1024 * 1024

low = jnp.bfloat16


def matmul(a, b):
    return lax.dot_general(a, b, (((1,), (0,)), ((), ())), preferred_element_type=jnp.float32)


def matmul_nt(a, b):
    return lax.dot_general(a, b, (((1,), (1,)), ((), ())), preferred_element_type=jnp.float32)


def cost(flops, *arrays):
    size = sum(a.size * a.dtype.itemsize for a in arrays)
    return pl.CostEstimate(flops=flops, bytes_accessed=size, transcendentals=0)


def half_rotation(blocks, rights, place, nb, parts, held):
    rows = blocks[0].shape[0]
    width = rights[0].shape[1] // parts
    count = len(blocks)

    def kernel(place_ref, *refs):
        lhs, rhs, outs = refs[:count], refs[count : 2 * count], refs[-parts:]
        for j, out in enumerate(outs):
            cols = slice(j * width, (j + 1) * width)
            total = matmul(lhs[0][...], rhs[0][:, cols])
            for i in range(1, count):
                total += matmul(lhs[i][...], rhs[i][:, cols])
            out[...] = total.astype(out.dtype)

    outs = [jax.ShapeDtypeStruct((nb * rows, width), low)] * parts
    return pl.pallas_call(
        kernel,
        out_shape=outs,
        grid_spec=pltpu.PrefetchScalarGridSpec(
            num_scalar_prefetch=1,
            grid=(1,),
            in_specs=[pl.BlockSpec(a.shape, lambda k, p: (0, 0)) for a in (*blocks, *rights)]
            + [pl.BlockSpec(memory_space=pl.ANY)] * len(held),
            out_specs=[pl.BlockSpec((rows, width), lambda k, p: (p[0], 0))] * parts,
        ),
        input_output_aliases={2 * count + 1 + j: j for j in range(len(held))},
        compiler_params=pltpu.CompilerParams(vmem_limit_bytes=VMEM_BYTES),
        cost_estimate=cost(2 * rows * sum(r.size for r in rights), *blocks, *rights),
        name="half_rotation",
    )(place, *blocks, *rights, *held)


def per_device(gradient, left_basis, right_basis, first_moment, second_moment, *, nb, nd):
    nz = nb
    nx = nd // nz
    b = lax.axis_index("basis")
    d = lax.axis_index("dp")
    z, x = d // nx, d % nx
    bits = [1 << k for k in range(nb.bit_length() - 1)]
    x_bits = [1 << k for k in range(nx.bit_length() - 1)]

    def permute(value, target):
        pairs = []
        for bb in range(nb):
            for zz in range(nz):
                for xx in range(nx):
                    tb, tz, tx = target(bb, zz, xx)
                    pairs.append((bb * nd + zz * nx + xx, tb * nd + tz * nx + tx))
        return lax.ppermute(value, ("basis", "dp"), pairs)

    def move_b(value, t):
        return permute(value, lambda bb, zz, xx: (bb ^ t, zz, xx))

    def move_z(value, t):
        return permute(value, lambda bb, zz, xx: (bb, zz ^ t, xx))

    def move_x(value, u):
        return permute(value, lambda bb, zz, xx: (bb, zz, xx ^ u))

    def spread(beta):
        return (beta >> 1) ^ ((beta & 1) * (nz - 1))

    unspread = [0] * nz
    for beta in range(nb):
        unspread[spread(beta)] = beta

    def joined(mine, other, bit_set, axis):
        first = jnp.where(bit_set, other, mine)
        second = jnp.where(bit_set, mine, other)
        return jnp.stack([first, second], axis=axis)

    def after(value, *others):
        return lax.optimization_barrier((value,) + others)[0]

    ff_block = right_basis.shape[1]
    rows = first_moment.shape[0]
    out_rows = left_basis.shape[1]
    whole = rows * nb

    order = [0]
    for t in reversed(bits):
        order = order + [s | t for s in order]
    half_places = [[[order.index(unspread[bb ^ zz ^ s] ^ bb) for s in range(nz)] for zz in range(nz)] for bb in range(nb)]
    half_places = jnp.array(half_places, jnp.int32)[b, z]
    uses = [(s, u) for s in reversed(range(nz)) for u in (*range(1, nx), 0)]
    order_of = jnp.array([order.index(t) for t in range(nb)], jnp.int32)
    use_places = [order_of[b ^ z ^ s] * rows + (x ^ u) * out_rows for s, u in uses]

    def together(*values):
        return lax.optimization_barrier(values)

    left_t = left_basis.astype(low).T
    right = right_basis.astype(low)

    def across(piece):
        return permute(piece, lambda bb, zz, xx: (bb, zz ^ spread(bb), xx))

    def along(piece):
        return permute(piece, lambda bb, zz, xx: (zz ^ spread(bb), zz, xx))

    ff_rows = right.shape[0] // nx
    right_parts = [lax.dynamic_slice_in_dim(right_basis, (x ^ u) * ff_rows, ff_rows, 0).astype(low) for u in range(nx)]

    piece = across(gradient)
    for i, t in enumerate(reversed(bits)):
        left_t = joined(left_t, move_z(left_t, t), (z & t) != 0, i)
    piece, left_t, half_places, *right_parts = together(piece, left_t, half_places, *right_parts)
    piece = along(piece)
    for i, u in enumerate(reversed(x_bits)):
        other, piece = together(move_x(left_t, u), piece)
        left_t = joined(left_t, other, (x & u) != 0, len(bits) + i)
    left_t = left_t.reshape(whole, rows)

    turns = sorted(range(nz), key=lambda s: (s.bit_count(), s))
    part = rows // 2
    parts = {(0, h): piece[h * part : (h + 1) * part] for h in range(2)}
    left_moves = [(t, h) for t in reversed(bits) for h in range(2)]
    left_got = []
    half = []
    for i, s in enumerate(turns):
        block = piece if not s else jnp.concatenate([parts[s, 0], parts[s, 1]], axis=0)
        group = {("x", u): move_x(block, u) for u in range(1, nx)}
        for k, h in ((i + 1, 0), (i + 1, 1), (i + 2, 0)):
            if k < nz and (turns[k], h) not in parts:
                t = turns[k]
                group[t, h] = move_z(parts[t & (t - 1), h], t & -t)
        while left_moves and (i == nz - 1 or "left" not in group) and i:
            t, h = left_moves.pop(0)
            group["left"] = move_b(left_t[h * whole // 2 : (h + 1) * whole // 2], t)
            left_got.append(group["left"])
            if i == nz - 1 and h:
                left_t = jnp.concatenate([left_t, jnp.concatenate(left_got[-2:], axis=0)], axis=1)
        names = list(group)
        group = dict(zip(names, together(*[group[name] for name in names])))
        if "left" in group and i < nz - 1:
            left_got[-1] = group["left"]
            if len(left_got) % 2 == 0:
                left_t = jnp.concatenate([left_t, jnp.concatenate(left_got[-2:], axis=0)], axis=1)
        parts.update({name: value for name, value in group.items() if name[0] not in ("x", "l")})
        row = [block] + [group["x", u] for u in range(1, nx)]
        half = list(half_rotation(row, right_parts, half_places[s : s + 1], nb, COL_PARTS, half))

    left = jnp.concatenate(
        [lax.dynamic_slice_in_dim(left_t, start, out_rows, 1).T for start in use_places], axis=0
    )
    left = lax.optimization_barrier(left)

    odd = sorted(range(1, nb, 2), key=lambda t: -t)
    groups = odd[: nb // 4], odd[nb // 4 :]
    turns = [(t ^ f, j) for group in groups for j in range(COL_PARTS) for t in group for f in (0, 1)]
    products = {}
    last = None
    for t, j in turns:
        rows_of = lax.dynamic_slice_in_dim(left_t, (b ^ t) * rows, rows, 0)
        part = half[j] if last is None else after(half[j], last)
        last = products[t, j] = lax.optimization_barrier(matmul(rows_of, part).astype(low))

    width = ff_block // COL_PARTS
    first_out, second_out, columns, joins = [], [], [], []
    for j in range(COL_PARTS):
        cols = slice(j * width, (j + 1) * width)
        held = {}
        for t in odd:
            held[t ^ 1] = products[t ^ 1, j].astype(jnp.float32) + move_b(products[t, j], 1).astype(jnp.float32)
        for t in reversed(bits[1:]):
            for s in [s for s in held if s & t]:
                away = held.pop(s).astype(low)
                if j:
                    away = after(away, summed)
                arrived = move_b(away, t)
                held[s ^ t] = held[s ^ t] + arrived.astype(jnp.float32)
        rotated, summed = held[0], arrived
        moments = first_moment[:, cols], second_moment[:, cols]
        if j:
            moments = after(moments, previous)
        first_new = beta_first * moments[0] + (1.0 - beta_first) * rotated
        second_new = beta_second * moments[1] + (1.0 - beta_second) * rotated * rotated
        first_fix = 1.0 - beta_first**STEP
        second_fix = 1.0 - beta_second**STEP
        direction = first_new / first_fix / (jnp.sqrt(second_new / second_fix) + epsilon)
        first_out.append(first_new)
        second_out.append(second_new)
        column = previous = direction.astype(low)
        axis = 0
        for t in reversed(bits):
            other = move_b(column, t)
            if j:
                other = after(other, joins[axis])
            column = joined(column, other, (b & t) != 0, axis)
            joins[axis : axis + 1] = [column]
            axis += 1
        columns.append(column.reshape(whole, width))

    columns = lax.optimization_barrier(jnp.concatenate(columns, axis=1))

    def partial(s, u):
        start = uses.index((s, u)) * out_rows
        back = lax.optimization_barrier(matmul(left[start : start + out_rows], columns).astype(low))
        return matmul_nt(back, right)

    arrived = {}
    for s in reversed(range(nz)):
        for u in range(1, nx):
            arrived[s, u] = move_x(partial(s, u).astype(low), u)
    sums = {}
    for s in reversed(range(nz)):
        total = partial(s, 0)
        for u in range(1, nx):
            total = total + arrived[s, u].astype(jnp.float32)
        t = 1
        while s % (2 * t) == 0 and t < nz:
            if s + t in sums:
                total = total + sums.pop(s + t).astype(jnp.float32)
            t *= 2
        sums[s] = move_z(total.astype(low), s & -s) if s else total
    return (
        jnp.concatenate(first_out, axis=1),
        jnp.concatenate(second_out, axis=1),
        sums[0].astype(low),
    )


def solution(mesh):
    nb, nd = mesh.shape["basis"], mesh.shape["dp"]

    return jax.shard_map(
        functools.partial(per_device, nb=nb, nd=nd),
        mesh=mesh,
        in_specs=(
            P("basis", "dp"),
            P("basis", "dp"),
            P("basis", "dp"),
            P("basis", "dp"),
            P("basis", "dp"),
        ),
        out_specs=(P("basis", "dp"), P("basis", "dp"), P("dp", "basis")),
        check_vma=False,
    )
```

```python
import functools

import jax
import jax.numpy as jnp
from jax import lax
from jax.experimental import pallas as pl
from jax.experimental.pallas import tpu as pltpu
from jax.sharding import PartitionSpec as P

STEP = 4


beta_first = 0.95
beta_second = 0.95
epsilon = 1e-08

COL_PARTS = 2

VMEM_BYTES = 54 * 1024 * 1024

low = jnp.bfloat16


def matmul(a, b):
    return lax.dot_general(a, b, (((1,), (0,)), ((), ())), preferred_element_type=jnp.float32)


def matmul_nt(a, b):
    return lax.dot_general(a, b, (((1,), (1,)), ((), ())), preferred_element_type=jnp.float32)


def cost(flops, *arrays):
    size = sum(a.size * a.dtype.itemsize for a in arrays)
    return pl.CostEstimate(flops=flops, bytes_accessed=size, transcendentals=0)


def half_rotation(gathered, right, places, nz, parts, part, row_parts, held):
    count, rows, cols = gathered.shape
    nx = count // nz
    width = right.shape[1] // parts

    def kernel(places_ref, *refs):
        blocks, right_ref, outs = refs[:nx], refs[nx], refs[-parts:]
        for j, out in enumerate(outs):
            total = matmul(blocks[0][...], right_ref[:cols, j * width : (j + 1) * width])
            for i in range(1, nx):
                total += matmul(blocks[i][...], right_ref[i * cols : (i + 1) * cols, j * width : (j + 1) * width])
            out[...] = total.astype(out.dtype)

    def block_of(i):
        if i % 2 == 0:
            return pl.BlockSpec((None, rows, cols), lambda k, p: (i * nz + k, 0, 0))
        return pl.BlockSpec((None, rows, cols), lambda k, p: (i * nz + nz - 1 - k, 0, 0))

    outs = [jax.ShapeDtypeStruct((nz * rows * row_parts, width), low)] * parts
    return pl.pallas_call(
        kernel,
        out_shape=outs,
        grid_spec=pltpu.PrefetchScalarGridSpec(
            num_scalar_prefetch=1,
            grid=(nz,),
            in_specs=[block_of(i) for i in range(nx)]
            + [pl.BlockSpec(right.shape, lambda k, p: (0, 0), pipeline_mode=pl.Buffered(1))]
            + [pl.BlockSpec(memory_space=pl.ANY)] * len(held),
            out_specs=[pl.BlockSpec((rows, width), lambda k, p: (p[k] * row_parts + part, 0))] * parts,
        ),
        input_output_aliases={nx + 2 + j: j for j in range(len(held))},
        compiler_params=pltpu.CompilerParams(vmem_limit_bytes=VMEM_BYTES),
        cost_estimate=cost(2 * gathered.size * right.shape[1], gathered, right, *outs),
        name="half_rotation",
    )(places, *([gathered] * nx), right, *held)


def per_device(gradient, left_basis, right_basis, first_moment, second_moment, *, nb, nd):
    nz = nb
    nx = nd // nz
    b = lax.axis_index("basis")
    d = lax.axis_index("dp")
    z, x = d // nx, d % nx
    bits = [1 << k for k in range(nb.bit_length() - 1)]
    x_bits = [1 << k for k in range(nx.bit_length() - 1)]

    def permute(value, target):
        pairs = []
        for bb in range(nb):
            for zz in range(nz):
                for xx in range(nx):
                    tb, tz, tx = target(bb, zz, xx)
                    pairs.append((bb * nd + zz * nx + xx, tb * nd + tz * nx + tx))
        return lax.ppermute(value, ("basis", "dp"), pairs)

    def move_b(value, t):
        return permute(value, lambda bb, zz, xx: (bb ^ t, zz, xx))

    def move_z(value, t):
        return permute(value, lambda bb, zz, xx: (bb, zz ^ t, xx))

    def move_x(value, u):
        return permute(value, lambda bb, zz, xx: (bb, zz, xx ^ u))

    def spread(beta):
        return (beta >> 1) ^ ((beta & 1) * (nz - 1))

    unspread = [0] * nz
    for beta in range(nb):
        unspread[spread(beta)] = beta

    def joined(mine, other, bit_set, axis):
        first = jnp.where(bit_set, other, mine)
        second = jnp.where(bit_set, mine, other)
        return jnp.stack([first, second], axis=axis)

    def after(value, *others):
        return lax.optimization_barrier((value,) + others)[0]

    ff_block = right_basis.shape[1]
    rows = first_moment.shape[0]
    out_rows = left_basis.shape[1]
    whole = rows * nb

    path = []
    for xx in range(nx):
        path += [zz * nx + xx for zz in (range(nz) if xx % 2 == 0 else reversed(range(nz)))]

    order = [0]
    for t in reversed(bits):
        order = order + [s | t for s in order]
    half_places = [[order.index(unspread[bb ^ zz] ^ bb) for zz in range(nz)] for bb in range(nb)]
    half_places = jnp.array(half_places, jnp.int32)[b]
    order_of = jnp.array([order.index(t) for t in range(nb)], jnp.int32)
    path_places = [order_of[b ^ (dd // nx)] * rows + dd % nx * out_rows for dd in path]

    def together(*values):
        return lax.optimization_barrier(values)

    left_t = left_basis.astype(low).T
    right = right_basis.astype(low)

    def across(piece):
        return permute(piece, lambda bb, zz, xx: (bb, zz ^ spread(bb), xx))

    def along(piece):
        return permute(piece, lambda bb, zz, xx: (zz ^ spread(bb), zz, xx))

    part = rows // 2
    first, second = gradient[:part], gradient[part:]
    first = across(first)
    for i, t in enumerate(reversed(bits[1:])):
        left_t = joined(left_t, move_z(left_t, t), (z & t) != 0, i)
    first, left_t, right, half_places = together(first, left_t, right, half_places)
    left_t = joined(left_t, move_z(left_t, bits[0]), (z & bits[0]) != 0, len(bits) - 1)
    first, second, left_t = together(along(first), across(after(second, first)), left_t)
    gathered = [lax.all_gather(first, "dp", axis_index_groups=[path])]
    second = along(second)
    for i, u in enumerate(reversed(x_bits)):
        other, second = together(move_x(left_t, u), second)
        left_t = joined(left_t, other, (x & u) != 0, len(bits) + i)
    gathered.append(lax.all_gather(second, "dp", axis_index_groups=[path]))
    left_t = left_t.reshape(whole, rows)
    for t in reversed(bits):
        left_t = jnp.concatenate([left_t, move_b(left_t, t)], axis=1)
    left_t, gathered[1] = together(left_t, gathered[1])
    half = []
    for h in range(2):
        half = list(half_rotation(gathered[h], right, half_places, nz, COL_PARTS, h, 2, half))

    products = {}
    last = None
    odd = sorted(range(1, nb, 2), key=lambda t: -t)
    held = [{} for _ in range(COL_PARTS)]
    for group in (odd[: nb // 4], odd[nb // 4 :]):
        for j in range(COL_PARTS):
            for t in (t for pair in group for t in (pair, pair ^ 1)):
                rows_of = lax.dynamic_slice_in_dim(left_t, (b ^ t) * rows, rows, 0)
                part = half[j] if last is None else after(half[j], last)
                last = products[t, j] = lax.optimization_barrier(matmul(rows_of, part).astype(low))
        for j in range(COL_PARTS):
            for t in group:
                got = move_b(products[t, j], 1)
                held[j][t ^ 1] = products[t ^ 1, j].astype(jnp.float32) + got.astype(jnp.float32)
        last = held[0][group[-1] ^ 1] = lax.optimization_barrier(held[0][group[-1] ^ 1].astype(low))
    held[0] = {t: value.astype(jnp.float32) for t, value in held[0].items()}

    arrived = []
    for j in range(COL_PARTS):
        for t in reversed(bits[1:]):
            for s in [s for s in held[j] if s & t]:
                away = held[j].pop(s).astype(low)
                if j:
                    away = after(away, arrived[j - 1])
                got = move_b(away, t)
                held[j][s ^ t] = held[j][s ^ t] + got.astype(jnp.float32)
        arrived.append(got)

    source = after(left_t, arrived[0])
    left = jnp.concatenate(
        [lax.dynamic_slice_in_dim(source, start, out_rows, 1).T for start in path_places], axis=0
    )
    left = lax.optimization_barrier(left)

    width = ff_block // COL_PARTS
    first_out, second_out, directions = [], [], []
    for j in range(COL_PARTS):
        cols = slice(j * width, (j + 1) * width)
        rotated = held[j][0]
        moments = first_moment[:, cols], second_moment[:, cols]
        if j:
            moments = after(moments, directions[-1])
        first_new = beta_first * moments[0] + (1.0 - beta_first) * rotated
        second_new = beta_second * moments[1] + (1.0 - beta_second) * rotated * rotated
        first_fix = 1.0 - beta_first**STEP
        second_fix = 1.0 - beta_second**STEP
        direction = first_new / first_fix / (jnp.sqrt(second_new / second_fix) + epsilon)
        first_out.append(first_new)
        second_out.append(second_new)
        directions.append(direction.astype(low))

    back, joins = [], []
    for j, column in enumerate(directions):
        for axis, t in enumerate(reversed(bits)):
            other = move_b(column, t)
            if j:
                other = after(other, joins[axis], back[-1])
            elif not axis:
                other = after(other, left, directions[-1])
            column = joined(column, other, (b & t) != 0, axis)
            joins[axis : axis + 1] = [column]
        column = lax.optimization_barrier(column.reshape(whole, width))
        back.append(lax.optimization_barrier(matmul(left, column).astype(low)))

    back = lax.optimization_barrier(jnp.concatenate(back, axis=1))
    total = matmul_nt(back, right).astype(low)
    update = lax.psum_scatter(total, "dp", scatter_dimension=0, axis_index_groups=[path], tiled=True)
    return (
        jnp.concatenate(first_out, axis=1),
        jnp.concatenate(second_out, axis=1),
        update,
    )


def solution(mesh):
    nb, nd = mesh.shape["basis"], mesh.shape["dp"]

    return jax.shard_map(
        functools.partial(per_device, nb=nb, nd=nd),
        mesh=mesh,
        in_specs=(
            P("basis", "dp"),
            P("basis", "dp"),
            P("basis", "dp"),
            P("basis", "dp"),
            P("basis", "dp"),
        ),
        out_specs=(P("basis", "dp"), P("basis", "dp"), P("dp", "basis")),
        check_vma=False,
    )
```

```python
import functools

import jax
import jax.numpy as jnp
from jax import lax
from jax.experimental import pallas as pl
from jax.experimental.pallas import tpu as pltpu
from jax.sharding import PartitionSpec as P

STEP = 4


beta_first = 0.95
beta_second = 0.95
epsilon = 1e-08

COL_PARTS = 2

VMEM_BYTES = 54 * 1024 * 1024

BLOCK = 256

low = jnp.bfloat16


def matmul(a, b):
    return lax.dot_general(a, b, (((1,), (0,)), ((), ())), preferred_element_type=jnp.float32)


def cost(flops, *arrays):
    size = sum(a.size * a.dtype.itemsize for a in arrays)
    return pl.CostEstimate(flops=flops, bytes_accessed=size, transcendentals=0)


def half_rotation(gathered, right, places, nz, parts, prior):
    count, rows, cols = gathered.shape
    nx = count // nz
    width = right.shape[1] // parts
    block = min(BLOCK, width)
    per = width // block
    halves = 2 if prior else 1

    def kernel(places_ref, blocks_ref, right_ref, *refs):
        prior_refs, outs = refs[:-parts], refs[-parts:]
        step = pl.program_id(0)
        totals = [
            matmul(blocks_ref[i * nz : (i + 1) * nz].reshape(nz * rows, cols), right_ref[i * cols : (i + 1) * cols])
            for i in range(nx)
        ]
        for j, out in enumerate(outs):

            @pl.when(step // per == j)
            def _():
                for k in range(nz):
                    total = totals[0][k * rows : (k + 1) * rows]
                    for i in range(1, nx):
                        at = k if i % 2 == 0 else nz - 1 - k
                        total = total + totals[i][at * rows : (at + 1) * rows]
                    total = total.astype(out.dtype)
                    if prior:
                        start = pl.multiple_of(places_ref[k] * (2 * rows), 2 * rows)
                        out[pl.ds(start, rows)] = prior_refs[j][k * rows : (k + 1) * rows]
                        out[pl.ds(start + rows, rows)] = total
                    else:
                        out[k * rows : (k + 1) * rows] = total

    def part_block(j, height):
        return pl.BlockSpec((height, block), lambda n, p: (0, jnp.clip(n - j * per, 0, per - 1)))

    outs = [jax.ShapeDtypeStruct((nz * rows * halves, width), low)] * parts
    return pl.pallas_call(
        kernel,
        out_shape=outs,
        grid_spec=pltpu.PrefetchScalarGridSpec(
            num_scalar_prefetch=1,
            grid=(parts * per,),
            in_specs=[
                pl.BlockSpec(gathered.shape, lambda n, p: (0, 0, 0), pipeline_mode=pl.Buffered(1)),
                pl.BlockSpec((nx * cols, block), lambda n, p: (0, n)),
            ]
            + [part_block(j, nz * rows) for j in range(len(prior))],
            out_specs=[part_block(j, nz * rows * halves) for j in range(parts)],
        ),
        compiler_params=pltpu.CompilerParams(vmem_limit_bytes=VMEM_BYTES),
        cost_estimate=cost(2 * gathered.size * right.shape[1], gathered, right, *outs),
        name="half_rotation",
    )(places, gathered, right, *prior)


def back_rotation(columns, right_t):
    parts = len(columns)
    rows, width = columns[0].shape
    block = min(BLOCK, right_t.shape[1])

    def kernel(*refs):
        rows_of, right_ref, out = refs[:parts], refs[parts], refs[parts + 1]
        total = matmul(rows_of[0][...], right_ref[:width])
        for j in range(1, parts):
            total += matmul(rows_of[j][...], right_ref[j * width : (j + 1) * width])
        out[...] = total.astype(out.dtype)

    out = jax.ShapeDtypeStruct((rows, right_t.shape[1]), low)
    return pl.pallas_call(
        kernel,
        out_shape=out,
        grid=(right_t.shape[1] // block,),
        in_specs=[pl.BlockSpec((rows, width), lambda n: (0, 0), pipeline_mode=pl.Buffered(1))] * parts
        + [pl.BlockSpec((right_t.shape[0], block), lambda n: (0, n))],
        out_specs=pl.BlockSpec((rows, block), lambda n: (0, n)),
        compiler_params=pltpu.CompilerParams(vmem_limit_bytes=VMEM_BYTES),
        cost_estimate=cost(2 * rows * right_t.size, right_t, out, *columns),
        name="back_rotation",
    )(*columns, right_t)


def per_device(gradient, left_basis, right_basis, first_moment, second_moment, *, nb, nd):
    nz = nb
    nx = nd // nz
    b = lax.axis_index("basis")
    d = lax.axis_index("dp")
    z, x = d // nx, d % nx
    bits = [1 << k for k in range(nb.bit_length() - 1)]
    x_bits = [1 << k for k in range(nx.bit_length() - 1)]

    def permute(value, target):
        pairs = []
        for bb in range(nb):
            for zz in range(nz):
                for xx in range(nx):
                    tb, tz, tx = target(bb, zz, xx)
                    pairs.append((bb * nd + zz * nx + xx, tb * nd + tz * nx + tx))
        return lax.ppermute(value, ("basis", "dp"), pairs)

    def move_b(value, t):
        return permute(value, lambda bb, zz, xx: (bb ^ t, zz, xx))

    def move_z(value, t):
        return permute(value, lambda bb, zz, xx: (bb, zz ^ t, xx))

    def move_x(value, u):
        return permute(value, lambda bb, zz, xx: (bb, zz, xx ^ u))

    def spread(beta):
        return (beta >> 1) ^ ((beta & 1) * (nz - 1))

    unspread = [0] * nz
    for beta in range(nb):
        unspread[spread(beta)] = beta

    def joined(mine, other, bit_set, axis):
        first = jnp.where(bit_set, other, mine)
        second = jnp.where(bit_set, mine, other)
        return jnp.stack([first, second], axis=axis)

    def after(value, *others):
        return lax.optimization_barrier((value,) + others)[0]

    ff_block = right_basis.shape[1]
    rows = first_moment.shape[0]
    out_rows = left_basis.shape[1]
    whole = rows * nb

    path = []
    for xx in range(nx):
        path += [zz * nx + xx for zz in (range(nz) if xx % 2 == 0 else reversed(range(nz)))]

    order = [0]
    for t in reversed(bits):
        order = order + [s | t for s in order]
    half_places = [[order.index(unspread[bb ^ zz] ^ bb) for zz in range(nz)] for bb in range(nb)]
    half_places = jnp.array(half_places, jnp.int32)[b]
    paths = [path if bb % 2 == 0 else path[::-1] for bb in range(nb)]
    groups = [[bb * nd + dd for dd in paths[bb]] for bb in range(nb)]
    path_places = [[order.index(bb ^ (dd // nx)) * rows + dd % nx * out_rows for dd in paths[bb]] for bb in range(nb)]
    path_places = jnp.array(path_places, jnp.int32)[b]

    def together(*values):
        return lax.optimization_barrier(values)

    left_t = left_basis.astype(low).T
    ff_rows = right_basis.shape[0] // nx
    first_x = (b & 1) * (nx - 1)
    right = jnp.concatenate(
        [
            lax.dynamic_slice_in_dim(right_basis, (first_x + (1 - 2 * (b & 1)) * i) * ff_rows, ff_rows, 0).astype(low)
            for i in range(nx)
        ],
        axis=0,
    )
    right_t = right_basis.astype(low).T

    def across(piece):
        return permute(piece, lambda bb, zz, xx: (bb, zz ^ spread(bb), xx))

    def along(piece):
        return permute(piece, lambda bb, zz, xx: (zz ^ spread(bb), zz, xx))

    part = rows // 2
    first, second = gradient[:part], gradient[part:]
    first = across(first)
    for i, t in enumerate(reversed(bits[1:])):
        left_t = joined(left_t, move_z(left_t, t), (z & t) != 0, i)
    first, left_t, right, half_places, path_places = together(first, left_t, right, half_places, path_places)
    left_t = joined(left_t, move_z(left_t, bits[0]), (z & bits[0]) != 0, len(bits) - 1)
    first, second, left_t = together(along(first), across(after(second, first)), left_t)
    gathered = [lax.all_gather(first, ("basis", "dp"), axis_index_groups=groups)]
    second = along(second)
    for i, u in enumerate(reversed(x_bits)):
        other, second = together(move_x(left_t, u), second)
        left_t = joined(left_t, other, (x & u) != 0, len(bits) + i)
    gathered.append(lax.all_gather(second, ("basis", "dp"), axis_index_groups=groups))
    left_t = left_t.reshape(whole, rows)
    for t in reversed(bits):
        left_t = jnp.concatenate([left_t, move_b(left_t, t)], axis=1)
    left_t, right_t, gathered[1] = together(left_t, right_t, gathered[1])
    half = []
    for h in range(2):
        half = half_rotation(gathered[h], right, half_places, nz, COL_PARTS, half)

    products = {}
    last = None
    odd = sorted(range(1, nb, 2), key=lambda t: -t)
    held = [{} for _ in range(COL_PARTS)]
    for group in (odd[: nb // 4], odd[nb // 4 :]):
        for j in range(COL_PARTS):
            for t in (t for pair in group for t in (pair, pair ^ 1)):
                rows_of = lax.dynamic_slice_in_dim(left_t, (b ^ t) * rows, rows, 0)
                part = half[j] if last is None else after(half[j], last)
                last = products[t, j] = lax.optimization_barrier(matmul(rows_of, part).astype(low))
        for j in range(COL_PARTS):
            for t in group:
                got = move_b(products[t, j], 1)
                held[j][t ^ 1] = products[t ^ 1, j].astype(jnp.float32) + got.astype(jnp.float32)
        last = held[0][group[-1] ^ 1] = lax.optimization_barrier(held[0][group[-1] ^ 1].astype(low))
    held[0] = {t: value.astype(jnp.float32) for t, value in held[0].items()}

    arrived = []
    for j in range(COL_PARTS):
        for t in reversed(bits[1:]):
            for s in [s for s in held[j] if s & t]:
                away = held[j].pop(s).astype(low)
                if j:
                    away = after(away, arrived[j - 1])
                got = move_b(away, t)
                held[j][s ^ t] = held[j][s ^ t] + got.astype(jnp.float32)
        arrived.append(got)

    source = after(left_t, arrived[0])
    left = jnp.concatenate(
        [lax.dynamic_slice_in_dim(source, path_places[i], out_rows, 1).T for i in range(nd)], axis=0
    )
    left = lax.optimization_barrier(left)

    width = ff_block // COL_PARTS
    first_out, second_out, directions = [], [], []
    for j in range(COL_PARTS):
        cols = slice(j * width, (j + 1) * width)
        rotated = held[j][0]
        moments = first_moment[:, cols], second_moment[:, cols]
        if j:
            moments = after(moments, directions[-1])
        first_new = beta_first * moments[0] + (1.0 - beta_first) * rotated
        second_new = beta_second * moments[1] + (1.0 - beta_second) * rotated * rotated
        first_fix = 1.0 - beta_first**STEP
        second_fix = 1.0 - beta_second**STEP
        direction = first_new / first_fix / (jnp.sqrt(second_new / second_fix) + epsilon)
        first_out.append(first_new)
        second_out.append(second_new)
        directions.append(direction.astype(low))

    back, joins = [], []
    for j, column in enumerate(directions):
        for axis, t in enumerate(reversed(bits)):
            other = move_b(column, t)
            if j:
                other = after(other, joins[axis], back[-1])
            elif not axis:
                other = after(other, left, directions[-1])
            column = joined(column, other, (b & t) != 0, axis)
            joins[axis : axis + 1] = [column]
        column = lax.optimization_barrier(column.reshape(whole, width))
        back.append(lax.optimization_barrier(matmul(left, column).astype(low)))

    total = back_rotation(back, right_t)
    update = lax.psum_scatter(total, ("basis", "dp"), scatter_dimension=0, axis_index_groups=groups, tiled=True)
    return (
        jnp.concatenate(first_out, axis=1),
        jnp.concatenate(second_out, axis=1),
        update,
    )


def solution(mesh):
    nb, nd = mesh.shape["basis"], mesh.shape["dp"]

    return jax.shard_map(
        functools.partial(per_device, nb=nb, nd=nd),
        mesh=mesh,
        in_specs=(
            P("basis", "dp"),
            P("basis", "dp"),
            P("basis", "dp"),
            P("basis", "dp"),
            P("basis", "dp"),
        ),
        out_specs=(P("basis", "dp"), P("basis", "dp"), P("dp", "basis")),
        check_vma=False,
    )
```

```python
import functools

import jax
import jax.numpy as jnp
from jax import lax
from jax.sharding import PartitionSpec as P

STEP = 4


beta_first = 0.95
beta_second = 0.95
epsilon = 1e-08

COL_PARTS = 2

low = jnp.bfloat16


def matmul(a, b):
    return lax.dot_general(a, b, (((1,), (0,)), ((), ())), preferred_element_type=jnp.float32)


def matmul_nt(a, b):
    return lax.dot_general(a, b, (((1,), (1,)), ((), ())), preferred_element_type=jnp.float32)


def per_device(gradient, left_basis, right_basis, first_moment, second_moment, *, nb, nd):
    nz = nb
    nx = nd // nz
    b = lax.axis_index("basis")
    bits = [1 << k for k in range(nb.bit_length() - 1)]

    def permute(value, target):
        pairs = []
        for bb in range(nb):
            for zz in range(nz):
                for xx in range(nx):
                    tb, tz, tx = target(bb, zz, xx)
                    pairs.append((bb * nd + zz * nx + xx, tb * nd + tz * nx + tx))
        return lax.ppermute(value, ("basis", "dp"), pairs)

    def move_b(value, t):
        return permute(value, lambda bb, zz, xx: (bb ^ t, zz, xx))

    def spread(beta):
        return (beta >> 1) ^ ((beta & 1) * (nz - 1))

    unspread = [0] * nz
    for beta in range(nb):
        unspread[spread(beta)] = beta

    def joined(mine, other, bit_set, axis):
        first = jnp.where(bit_set, other, mine)
        second = jnp.where(bit_set, mine, other)
        return jnp.stack([first, second], axis=axis)

    def after(value, *others):
        return lax.optimization_barrier((value,) + others)[0]

    ff_block = right_basis.shape[1]
    rows = first_moment.shape[0]
    out_rows = left_basis.shape[1]
    whole = rows * nb

    path = []
    for xx in range(nx):
        path += [zz * nx + xx for zz in (range(nz) if xx % 2 == 0 else reversed(range(nz)))]

    order = [0]
    for t in reversed(bits):
        order = order + [s | t for s in order]
    half_places = [[order.index(unspread[bb ^ zz] ^ bb) * rows for zz in range(nz)] for bb in range(nb)]
    path_places = [[order.index(bb ^ (dd // nx)) * rows + dd % nx * out_rows for dd in path] for bb in range(nb)]
    half_places = jnp.array(half_places, jnp.int32)[b]
    path_places = jnp.array(path_places, jnp.int32)[b]

    def together(*values):
        return lax.optimization_barrier(values)

    def round_path(value):
        return lax.all_gather(value, "dp", axis_index_groups=[path])

    width = ff_block // COL_PARTS
    right = right_basis.astype(low)
    ff_rows = right.shape[0] // nx
    right_parts = [
        [right_basis[i * ff_rows : (i + 1) * ff_rows, j * width : (j + 1) * width].astype(low) for i in range(nx)]
        for j in range(COL_PARTS)
    ]

    left_blocks = round_path(left_basis.astype(low).T)
    piece = permute(gradient, lambda bb, zz, xx: (bb, zz ^ spread(bb), xx))
    piece, half_places, path_places, right_parts = together(piece, half_places, path_places, right_parts)
    piece = permute(piece, lambda bb, zz, xx: (zz ^ spread(bb), zz, xx))
    part = rows // 2
    piece, left_blocks = together(piece, left_blocks)
    gathered = [round_path(piece[h * part : (h + 1) * part]) for h in range(2)]

    left_t = jnp.concatenate([left_blocks[path.index(dd)] for dd in range(nd)], axis=0)
    for t in reversed(bits):
        left_t = jnp.concatenate([left_t, move_b(left_t, t)], axis=1)
    left_t = lax.optimization_barrier(left_t)
    left_halves = [
        lax.optimization_barrier(
            jnp.concatenate(
                [lax.dynamic_slice_in_dim(left_t, half_places[zz] + h * part, part, 1) for zz in range(nz)], axis=1
            )
        )
        for h in range(2)
    ]

    def columns_of(blocks):
        found = []
        for i in range(nx):
            mine = blocks[i * nz : (i + 1) * nz]
            mine = mine if i % 2 == 0 else jnp.flip(mine, 0)
            found.append(mine.reshape(nz * part, ff_rows))
        return lax.optimization_barrier(found)

    def half_rotation(found, j):
        total = sum(matmul(mine, right_parts[j][i]) for i, mine in enumerate(found))
        return lax.optimization_barrier(total.astype(low))

    def product(t, h, value):
        return matmul(lax.dynamic_slice_in_dim(left_halves[h], (b ^ t) * rows, rows, 0), value)

    found = columns_of(gathered[0])
    half = [half_rotation(found, j) for j in range(COL_PARTS)]
    early = {(t, j): product(t, 0, half[j]) for j in range(COL_PARTS) for t in range(nb)}
    names = list(early)
    gathered[1], *values = together(gathered[1], *[early[name] for name in names])
    early = dict(zip(names, values))
    found = columns_of(gathered[1])
    half = [None] * COL_PARTS

    products = {}
    last = None
    odd = sorted(range(1, nb, 2), key=lambda t: -t)
    held = [{} for _ in range(COL_PARTS)]
    for group in (odd[: nb // 4], odd[nb // 4 :]):
        for j in range(COL_PARTS):
            for t in (t for pair in group for t in (pair, pair ^ 1)):
                if half[j] is None:
                    half[j] = half_rotation(found if last is None else after(found, last), j)
                value = half[j] if last is None else after(half[j], last)
                last = products[t, j] = lax.optimization_barrier((early[t, j] + product(t, 1, value)).astype(low))
        for j in range(COL_PARTS):
            for t in group:
                got = move_b(products[t, j], 1)
                held[j][t ^ 1] = products[t ^ 1, j].astype(jnp.float32) + got.astype(jnp.float32)
        last = held[0][group[-1] ^ 1] = lax.optimization_barrier(held[0][group[-1] ^ 1].astype(low))
    held[0] = {t: value.astype(jnp.float32) for t, value in held[0].items()}

    arrived = []
    for j in range(COL_PARTS):
        for t in reversed(bits[1:]):
            for s in [s for s in held[j] if s & t]:
                away = held[j].pop(s).astype(low)
                if j:
                    away = after(away, arrived[j - 1])
                got = move_b(away, t)
                held[j][s ^ t] = held[j][s ^ t] + got.astype(jnp.float32)
        arrived.append(got)

    source = after(left_t, arrived[0])
    left = jnp.concatenate(
        [lax.dynamic_slice_in_dim(source, path_places[i], out_rows, 1).T for i in range(nd)], axis=0
    )
    left = lax.optimization_barrier(left)

    first_out, second_out, directions = [], [], []
    for j in range(COL_PARTS):
        cols = slice(j * width, (j + 1) * width)
        rotated = held[j][0]
        moments = first_moment[:, cols], second_moment[:, cols]
        if j:
            moments = after(moments, directions[-1])
        first_new = beta_first * moments[0] + (1.0 - beta_first) * rotated
        second_new = beta_second * moments[1] + (1.0 - beta_second) * rotated * rotated
        first_fix = 1.0 - beta_first**STEP
        second_fix = 1.0 - beta_second**STEP
        direction = first_new / first_fix / (jnp.sqrt(second_new / second_fix) + epsilon)
        first_out.append(first_new)
        second_out.append(second_new)
        directions.append(direction.astype(low))

    back, joins = [], []
    for j, column in enumerate(directions):
        for axis, t in enumerate(reversed(bits)):
            other = move_b(column, t)
            if j:
                other = after(other, joins[axis], back[-1])
            elif not axis:
                other = after(other, left, directions[-1])
            column = joined(column, other, (b & t) != 0, axis)
            joins[axis : axis + 1] = [column]
        column = lax.optimization_barrier(column.reshape(whole, width))
        back.append(lax.optimization_barrier(matmul(left, column).astype(low)))

    back = lax.optimization_barrier(jnp.concatenate(back, axis=1))
    total = matmul_nt(back, right).astype(low)
    update = lax.psum_scatter(total, "dp", scatter_dimension=0, axis_index_groups=[path], tiled=True)
    return (
        jnp.concatenate(first_out, axis=1),
        jnp.concatenate(second_out, axis=1),
        update,
    )


def solution(mesh):
    nb, nd = mesh.shape["basis"], mesh.shape["dp"]

    return jax.shard_map(
        functools.partial(per_device, nb=nb, nd=nd),
        mesh=mesh,
        in_specs=(
            P("basis", "dp"),
            P("basis", "dp"),
            P("basis", "dp"),
            P("basis", "dp"),
            P("basis", "dp"),
        ),
        out_specs=(P("basis", "dp"), P("basis", "dp"), P("dp", "basis")),
        check_vma=False,
    )
```

```python
import functools

import jax
import jax.numpy as jnp
from jax import lax
from jax.sharding import PartitionSpec as P

STEP = 4


beta_first = 0.95
beta_second = 0.95
epsilon = 1e-08

COL_PARTS = 2

low = jnp.bfloat16


def matmul(a, b):
    return lax.dot_general(a, b, (((1,), (0,)), ((), ())), preferred_element_type=jnp.float32)


def matmul_nt(a, b):
    return lax.dot_general(a, b, (((1,), (1,)), ((), ())), preferred_element_type=jnp.float32)


def per_device(gradient, left_basis, right_basis, first_moment, second_moment, *, nb, nd):
    nz = nb
    nx = nd // nz
    b = lax.axis_index("basis")
    bits = [1 << k for k in range(nb.bit_length() - 1)]

    def permute(value, target):
        pairs = []
        for bb in range(nb):
            for zz in range(nz):
                for xx in range(nx):
                    tb, tz, tx = target(bb, zz, xx)
                    pairs.append((bb * nd + zz * nx + xx, tb * nd + tz * nx + tx))
        return lax.ppermute(value, ("basis", "dp"), pairs)

    def move_b(value, t):
        return permute(value, lambda bb, zz, xx: (bb ^ t, zz, xx))

    def spread(beta):
        return (beta >> 1) ^ ((beta & 1) * (nz - 1))

    def unspread(w):
        odd = (w >> (len(bits) - 1)) & 1
        return (w ^ (odd * (nz - 1))) * 2 + odd

    def joined(mine, other, bit_set, axis):
        first = jnp.where(bit_set, other, mine)
        second = jnp.where(bit_set, mine, other)
        return jnp.stack([first, second], axis=axis)

    def after(value, *others):
        return lax.optimization_barrier((value,) + others)[0]

    ff_block = right_basis.shape[1]
    rows = first_moment.shape[0]
    out_rows = left_basis.shape[1]
    whole = rows * nb

    path = []
    for xx in range(nx):
        path += [zz * nx + xx for zz in (range(nz) if xx % 2 == 0 else reversed(range(nz)))]

    def reversed_bits(t):
        return sum(((t >> k) & 1) << (len(bits) - 1 - k) for k in range(len(bits)))

    def together(*values):
        return lax.optimization_barrier(values)

    def round_path(value):
        return lax.all_gather(value, "dp", axis_index_groups=[path])

    width = ff_block // COL_PARTS
    right = right_basis.astype(low)
    ff_rows = right.shape[0] // nx
    right_parts = [
        [right_basis[i * ff_rows : (i + 1) * ff_rows, j * width : (j + 1) * width].astype(low) for i in range(nx)]
        for j in range(COL_PARTS)
    ]

    left_blocks = round_path(left_basis.astype(low).T)
    piece = permute(gradient, lambda bb, zz, xx: (bb, zz ^ spread(bb), xx))
    piece, right_parts = together(piece, right_parts)
    piece = permute(piece, lambda bb, zz, xx: (zz ^ spread(bb), zz, xx))
    piece, left_blocks = together(piece, left_blocks)
    gathered = round_path(piece)

    left_t = jnp.concatenate([left_blocks[path.index(dd)] for dd in range(nd)], axis=0)
    for t in reversed(bits):
        left_t = jnp.concatenate([left_t, move_b(left_t, t)], axis=1)
    left_t = lax.optimization_barrier(left_t)
    left_rows = jnp.concatenate(
        [
            lax.dynamic_slice_in_dim(left_t, reversed_bits(unspread(b ^ zz) ^ b) * rows, rows, 1)
            for zz in range(nz)
        ],
        axis=1,
    )
    left_rows, gathered = together(left_rows, gathered)

    blocks = []
    for i in range(nx):
        mine = gathered[i * nz : (i + 1) * nz]
        mine = mine if i % 2 == 0 else jnp.flip(mine, 0)
        blocks.append(mine.reshape(whole, ff_rows))
    blocks = lax.optimization_barrier(blocks)
    half = [None] * COL_PARTS

    products = {}
    last = None
    odd = sorted(range(1, nb, 2), key=lambda t: -t)
    held = [{} for _ in range(COL_PARTS)]
    for group in (odd[: nb // 4], odd[nb // 4 :]):
        for j in range(COL_PARTS):
            for t in (t for pair in group for t in (pair, pair ^ 1)):
                if half[j] is None:
                    found = blocks if last is None else after(blocks, last)
                    total = sum(matmul(mine, right_parts[j][i]) for i, mine in enumerate(found))
                    half[j] = lax.optimization_barrier(total.astype(low))
                value = half[j] if last is None else after(half[j], last)
                rows_of = lax.dynamic_slice_in_dim(left_rows, (b ^ t) * rows, rows, 0)
                last = products[t, j] = lax.optimization_barrier(matmul(rows_of, value).astype(low))
        for j in range(COL_PARTS):
            for t in group:
                got = move_b(products[t, j], 1)
                held[j][t ^ 1] = products[t ^ 1, j].astype(jnp.float32) + got.astype(jnp.float32)
        last = held[0][group[-1] ^ 1] = lax.optimization_barrier(held[0][group[-1] ^ 1].astype(low))
    held[0] = {t: value.astype(jnp.float32) for t, value in held[0].items()}

    arrived = []
    for j in range(COL_PARTS):
        for t in reversed(bits[1:]):
            for s in [s for s in held[j] if s & t]:
                away = held[j].pop(s).astype(low)
                if j:
                    away = after(away, arrived[j - 1])
                got = move_b(away, t)
                held[j][s ^ t] = held[j][s ^ t] + got.astype(jnp.float32)
        arrived.append(got)

    source = after(left_t, arrived[0])
    left = jnp.concatenate(
        [
            lax.dynamic_slice_in_dim(
                source, reversed_bits(b ^ (dd // nx)) * rows + dd % nx * out_rows, out_rows, 1
            ).T
            for dd in path
        ],
        axis=0,
    )
    left = lax.optimization_barrier(left)

    first_out, second_out, directions = [], [], []
    for j in range(COL_PARTS):
        cols = slice(j * width, (j + 1) * width)
        rotated = held[j][0]
        moments = first_moment[:, cols], second_moment[:, cols]
        if j:
            moments = after(moments, directions[-1])
        first_new = beta_first * moments[0] + (1.0 - beta_first) * rotated
        second_new = beta_second * moments[1] + (1.0 - beta_second) * rotated * rotated
        first_fix = 1.0 - beta_first**STEP
        second_fix = 1.0 - beta_second**STEP
        direction = first_new / first_fix / (jnp.sqrt(second_new / second_fix) + epsilon)
        first_out.append(first_new)
        second_out.append(second_new)
        directions.append(direction.astype(low))

    columns, joins = [], []
    for j, column in enumerate(directions):
        for axis, t in enumerate(reversed(bits)):
            other = move_b(column, t)
            if j:
                other = after(other, joins[axis])
            column = joined(column, other, (b & t) != 0, axis)
            joins[axis : axis + 1] = [column]
        columns.append(column.reshape(whole, width))

    columns = lax.optimization_barrier(jnp.concatenate(columns, axis=1))
    back = lax.optimization_barrier(matmul(left, columns).astype(low))
    total = matmul_nt(back, right).astype(low)
    update = lax.psum_scatter(total, "dp", scatter_dimension=0, axis_index_groups=[path], tiled=True)
    return (
        jnp.concatenate(first_out, axis=1),
        jnp.concatenate(second_out, axis=1),
        update,
    )


def solution(mesh):
    nb, nd = mesh.shape["basis"], mesh.shape["dp"]

    return jax.shard_map(
        functools.partial(per_device, nb=nb, nd=nd),
        mesh=mesh,
        in_specs=(
            P("basis", "dp"),
            P("basis", "dp"),
            P("basis", "dp"),
            P("basis", "dp"),
            P("basis", "dp"),
        ),
        out_specs=(P("basis", "dp"), P("basis", "dp"), P("dp", "basis")),
        check_vma=False,
    )
```

```python
import functools

import jax
import jax.numpy as jnp
from jax import lax
from jax.sharding import PartitionSpec as P

STEP = 4


beta_first = 0.95
beta_second = 0.95
epsilon = 1e-08

COL_PARTS = 2

low = jnp.bfloat16


def matmul(a, b):
    return lax.dot_general(a, b, (((1,), (0,)), ((), ())), preferred_element_type=jnp.float32)


def matmul_nt(a, b):
    return lax.dot_general(a, b, (((1,), (1,)), ((), ())), preferred_element_type=jnp.float32)


def per_device(gradient, left_basis, right_basis, first_moment, second_moment, *, nb, nd):
    nz = nb
    nx = nd // nz
    b = lax.axis_index("basis")
    bits = [1 << k for k in range(nb.bit_length() - 1)]

    def permute(value, target):
        pairs = []
        for bb in range(nb):
            for zz in range(nz):
                for xx in range(nx):
                    tb, tz, tx = target(bb, zz, xx)
                    pairs.append((bb * nd + zz * nx + xx, tb * nd + tz * nx + tx))
        return lax.ppermute(value, ("basis", "dp"), pairs)

    def move_b(value, t):
        return permute(value, lambda bb, zz, xx: (bb ^ t, zz, xx))

    def spread(beta):
        return (beta >> 1) ^ ((beta & 1) * (nz - 1))

    def unspread(w):
        odd = (w >> (len(bits) - 1)) & 1
        return (w ^ (odd * (nz - 1))) * 2 + odd

    def joined(mine, other, bit_set, axis):
        first = jnp.where(bit_set, other, mine)
        second = jnp.where(bit_set, mine, other)
        return jnp.stack([first, second], axis=axis)

    def after(value, *others):
        return lax.optimization_barrier((value,) + others)[0]

    ff_block = right_basis.shape[1]
    rows = first_moment.shape[0]
    out_rows = left_basis.shape[1]
    whole = rows * nb

    path = []
    for xx in range(nx):
        path += [zz * nx + xx for zz in (range(nz) if xx % 2 == 0 else reversed(range(nz)))]

    def reversed_bits(t):
        return sum(((t >> k) & 1) << (len(bits) - 1 - k) for k in range(len(bits)))

    def together(*values):
        return lax.optimization_barrier(values)

    def round_path(value):
        return lax.all_gather(value, "dp", axis_index_groups=[path], tiled=True)

    width = ff_block // COL_PARTS
    right = right_basis.astype(low)
    ff_rows = right.shape[0] // nx
    right_parts = [
        [right_basis[i * ff_rows : (i + 1) * ff_rows, j * width : (j + 1) * width].astype(low) for i in range(nx)]
        for j in range(COL_PARTS)
    ]

    left_blocks = round_path(left_basis.astype(low).T)
    piece = permute(gradient, lambda bb, zz, xx: (bb, zz ^ spread(bb), xx))
    piece, right_parts = together(piece, right_parts)
    piece = permute(piece, lambda bb, zz, xx: (zz ^ spread(bb), zz, xx))
    piece, left_blocks = together(piece, left_blocks)
    gathered = round_path(piece)

    left_blocks = left_blocks.reshape(nd, out_rows, rows)
    left_t = jnp.concatenate([left_blocks[path.index(dd)] for dd in range(nd)], axis=0)
    for t in reversed(bits):
        left_t = jnp.concatenate([left_t, move_b(left_t, t)], axis=1)
    left_t = lax.optimization_barrier(left_t)
    left_rows = jnp.concatenate(
        [
            lax.dynamic_slice_in_dim(left_t, reversed_bits(unspread(b ^ zz) ^ b) * rows, rows, 1)
            for zz in range(nz)
        ],
        axis=1,
    )
    left_rows, gathered = together(left_rows, gathered)

    def half_rotation(gathered, j):
        total = None
        for i in range(nx):
            mine = gathered[i * whole : (i + 1) * whole]
            term = matmul(mine, right_parts[j][i])
            if i % 2:
                term = lax.optimization_barrier(term).reshape(nz, rows, width)
                term = jnp.flip(term, 0).reshape(whole, width)
            total = term if total is None else total + term
        return lax.optimization_barrier(total.astype(low))

    odd = sorted(range(1, nb, 2), key=lambda t: -t)
    first_group, second_group = odd[: nb // 4], odd[nb // 4 :]
    top = bits[-1]
    last = None

    def paired(t, j):
        nonlocal last
        values = []
        for u in (t, t ^ 1):
            value = half[j] if last is None else after(half[j], last)
            rows_of = lax.dynamic_slice_in_dim(left_rows, (b ^ u) * rows, rows, 0)
            last = lax.optimization_barrier(matmul(rows_of, value).astype(low))
            values.append(last)
        return values[1].astype(jnp.float32) + move_b(values[0], 1).astype(jnp.float32)

    half, arrived = [], []
    for j in range(COL_PARTS):
        half.append(half_rotation(gathered if last is None else after(gathered, last), j))
        away = [lax.optimization_barrier(paired(t, j).astype(low)) for t in first_group]
        last = away[-1]
        if j:
            away = [after(value, arrived[j - 1][-1]) for value in away]
        arrived.append([move_b(value, top) for value in away])
    last = after(arrived[0][-1], last)
    sums = []
    for j in range(COL_PARTS):
        held = {t ^ 1: paired(t, j) for t in second_group}
        for t, got in zip(first_group, arrived[j]):
            held[t ^ 1 ^ top] = held[t ^ 1 ^ top] + got.astype(jnp.float32)
        for t in reversed(bits[1:-1]):
            for s in [s for s in held if s & t]:
                held[s ^ t] = held[s ^ t] + move_b(held.pop(s).astype(low), t).astype(jnp.float32)
        sums.append(held[0])

    source = after(left_t, arrived[-1][-1])
    left = jnp.concatenate(
        [
            lax.dynamic_slice_in_dim(
                source, reversed_bits(b ^ (dd // nx)) * rows + dd % nx * out_rows, out_rows, 1
            ).T
            for dd in path
        ],
        axis=0,
    )
    left = lax.optimization_barrier(left)

    first_out, second_out, directions = [], [], []
    for j in range(COL_PARTS):
        cols = slice(j * width, (j + 1) * width)
        rotated = sums[j]
        moments = first_moment[:, cols], second_moment[:, cols]
        if j:
            moments = after(moments, directions[-1])
        first_new = beta_first * moments[0] + (1.0 - beta_first) * rotated
        second_new = beta_second * moments[1] + (1.0 - beta_second) * rotated * rotated
        first_fix = 1.0 - beta_first**STEP
        second_fix = 1.0 - beta_second**STEP
        direction = first_new / first_fix / (jnp.sqrt(second_new / second_fix) + epsilon)
        first_out.append(first_new)
        second_out.append(second_new)
        directions.append(direction.astype(low))

    columns, joins = [], []
    for j, column in enumerate(directions):
        for axis, t in enumerate(reversed(bits)):
            other = move_b(column, t)
            if j:
                other = after(other, joins[axis])
            column = joined(column, other, (b & t) != 0, axis)
            joins[axis : axis + 1] = [column]
        columns.append(column.reshape(whole, width))

    columns = lax.optimization_barrier(jnp.concatenate(columns, axis=1))
    back = lax.optimization_barrier(matmul(left, columns).astype(low))
    total = matmul_nt(back, right).astype(low)
    update = lax.psum_scatter(total, "dp", scatter_dimension=0, axis_index_groups=[path], tiled=True)
    return (
        jnp.concatenate(first_out, axis=1),
        jnp.concatenate(second_out, axis=1),
        update,
    )


def solution(mesh):
    nb, nd = mesh.shape["basis"], mesh.shape["dp"]

    return jax.shard_map(
        functools.partial(per_device, nb=nb, nd=nd),
        mesh=mesh,
        in_specs=(
            P("basis", "dp"),
            P("basis", "dp"),
            P("basis", "dp"),
            P("basis", "dp"),
            P("basis", "dp"),
        ),
        out_specs=(P("basis", "dp"), P("basis", "dp"), P("dp", "basis")),
        check_vma=False,
    )
```

```python
import functools

import jax
import jax.numpy as jnp
from jax import lax
from jax.experimental import pallas as pl
from jax.experimental.pallas import tpu as pltpu
from jax.sharding import PartitionSpec as P

STEP = 4


beta_first = 0.95
beta_second = 0.95
epsilon = 1e-08

COL_PARTS = 2

VMEM_BYTES = 52 * 1024 * 1024

low = jnp.bfloat16


def matmul(a, b):
    return lax.dot_general(a, b, (((1,), (0,)), ((), ())), preferred_element_type=jnp.float32)


def matmul_nt(a, b):
    return lax.dot_general(a, b, (((1,), (1,)), ((), ())), preferred_element_type=jnp.float32)


def half_rotation(gathered, right, places, nz):
    count, rows, cols = gathered.shape
    nx = count // nz
    width = right.shape[1]

    def kernel(places_ref, *refs):
        blocks, right_ref, out = refs[:nx], refs[nx], refs[nx + 1]
        total = matmul(blocks[0][...], right_ref[:cols])
        for i in range(1, nx):
            total += matmul(blocks[i][...], right_ref[i * cols : (i + 1) * cols])
        out[...] = total.astype(out.dtype)

    def block_of(i):
        if i % 2 == 0:
            return pl.BlockSpec((None, rows, cols), lambda k, p: (i * nz + k, 0, 0))
        return pl.BlockSpec((None, rows, cols), lambda k, p: (i * nz + nz - 1 - k, 0, 0))

    out = jax.ShapeDtypeStruct((nz * rows, width), low)
    size = sum(a.size * a.dtype.itemsize for a in (gathered, right, out))
    return pl.pallas_call(
        kernel,
        out_shape=out,
        grid_spec=pltpu.PrefetchScalarGridSpec(
            num_scalar_prefetch=1,
            grid=(nz,),
            in_specs=[block_of(i) for i in range(nx)]
            + [pl.BlockSpec(right.shape, lambda k, p: (0, 0), pipeline_mode=pl.Buffered(1))],
            out_specs=pl.BlockSpec((rows, width), lambda k, p: (p[k], 0)),
        ),
        compiler_params=pltpu.CompilerParams(vmem_limit_bytes=VMEM_BYTES),
        cost_estimate=pl.CostEstimate(flops=2 * gathered.size * width, bytes_accessed=size, transcendentals=0),
        name="half_rotation",
    )(places, *([gathered] * nx), right)


def per_device(gradient, left_basis, right_basis, first_moment, second_moment, *, nb, nd):
    nz = nb
    nx = nd // nz
    b = lax.axis_index("basis")
    bits = [1 << k for k in range(nb.bit_length() - 1)]

    def permute(value, target):
        pairs = []
        for bb in range(nb):
            for zz in range(nz):
                for xx in range(nx):
                    tb, tz, tx = target(bb, zz, xx)
                    pairs.append((bb * nd + zz * nx + xx, tb * nd + tz * nx + tx))
        return lax.ppermute(value, ("basis", "dp"), pairs)

    def move_b(value, t):
        return permute(value, lambda bb, zz, xx: (bb ^ t, zz, xx))

    def spread(beta):
        return (beta >> 1) ^ ((beta & 1) * (nz - 1))

    def unspread(w):
        odd = (w >> (len(bits) - 1)) & 1
        return (w ^ (odd * (nz - 1))) * 2 + odd

    def joined(mine, other, bit_set, axis):
        first = jnp.where(bit_set, other, mine)
        second = jnp.where(bit_set, mine, other)
        return jnp.stack([first, second], axis=axis)

    def after(value, *others):
        return lax.optimization_barrier((value,) + others)[0]

    ff_block = right_basis.shape[1]
    rows = first_moment.shape[0]
    out_rows = left_basis.shape[1]
    whole = rows * nb

    path = []
    for xx in range(nx):
        path += [zz * nx + xx for zz in (range(nz) if xx % 2 == 0 else reversed(range(nz)))]

    def reversed_bits(t):
        return sum(((t >> k) & 1) << (len(bits) - 1 - k) for k in range(len(bits)))

    def together(*values):
        return lax.optimization_barrier(values)

    def round_path(value):
        return lax.all_gather(value, "dp", axis_index_groups=[path], tiled=True)

    width = ff_block // COL_PARTS
    right = right_basis.astype(low)
    right_parts = [right_basis[:, j * width : (j + 1) * width].astype(low) for j in range(COL_PARTS)]
    places = jnp.stack([reversed_bits(unspread(b ^ zz) ^ b) for zz in range(nz)]).astype(jnp.int32)

    left_blocks = round_path(left_basis.astype(low).T)
    piece = permute(gradient, lambda bb, zz, xx: (bb, zz ^ spread(bb), xx))
    piece, right_parts, places = together(piece, right_parts, places)
    piece = permute(piece, lambda bb, zz, xx: (zz ^ spread(bb), zz, xx))
    piece, left_blocks = together(piece, left_blocks)
    gathered = round_path(piece)

    left_blocks = left_blocks.reshape(nd, out_rows, rows)
    left_t = jnp.concatenate([left_blocks[path.index(dd)] for dd in range(nd)], axis=0)
    for t in reversed(bits):
        left_t = jnp.concatenate([left_t, move_b(left_t, t)], axis=1)
    left_t, gathered = together(left_t, gathered.reshape(nd, rows, ff_block))

    odd = sorted(range(1, nb, 2), key=lambda t: -t)
    first_group, second_group = odd[: nb // 4], odd[nb // 4 :]
    top = bits[-1]
    last = None

    def paired(t, j):
        nonlocal last
        values = []
        for u in (t, t ^ 1):
            value = half[j] if last is None else after(half[j], last)
            rows_of = lax.dynamic_slice_in_dim(left_t, (b ^ u) * rows, rows, 0)
            last = lax.optimization_barrier(matmul(rows_of, value).astype(low))
            values.append(last)
        return values[1].astype(jnp.float32) + move_b(values[0], 1).astype(jnp.float32)

    half, arrived = [], []
    for j in range(COL_PARTS):
        found = gathered if last is None else after(gathered, last)
        half.append(half_rotation(found, right_parts[j], places, nz))
        away = [lax.optimization_barrier(paired(t, j).astype(low)) for t in first_group]
        last = away[-1]
        if j:
            away = [after(value, arrived[j - 1][-1]) for value in away]
        arrived.append([move_b(value, top) for value in away])
    last = arrived[0][-1]
    sums = []
    for j in range(COL_PARTS):
        held = {t ^ 1: paired(t, j) for t in second_group}
        for t, got in zip(first_group, arrived[j]):
            held[t ^ 1 ^ top] = held[t ^ 1 ^ top] + got.astype(jnp.float32)
        for t in reversed(bits[1:-1]):
            for s in [s for s in held if s & t]:
                held[s ^ t] = held[s ^ t] + move_b(held.pop(s).astype(low), t).astype(jnp.float32)
        sums.append(held[0])

    source = after(left_t, arrived[0][-1])
    left = jnp.concatenate(
        [
            lax.dynamic_slice_in_dim(
                source, reversed_bits(b ^ (dd // nx)) * rows + dd % nx * out_rows, out_rows, 1
            ).T
            for dd in path
        ],
        axis=0,
    )
    left = lax.optimization_barrier(left)

    first_out, second_out, directions = [], [], []
    for j in range(COL_PARTS):
        cols = slice(j * width, (j + 1) * width)
        rotated = sums[j]
        moments = first_moment[:, cols], second_moment[:, cols]
        if j:
            moments = after(moments, directions[-1])
        first_new = beta_first * moments[0] + (1.0 - beta_first) * rotated
        second_new = beta_second * moments[1] + (1.0 - beta_second) * rotated * rotated
        first_fix = 1.0 - beta_first**STEP
        second_fix = 1.0 - beta_second**STEP
        direction = first_new / first_fix / (jnp.sqrt(second_new / second_fix) + epsilon)
        first_out.append(first_new)
        second_out.append(second_new)
        directions.append(direction.astype(low))

    columns, joins = [], []
    for j, column in enumerate(directions):
        for axis, t in enumerate(reversed(bits)):
            other = move_b(column, t)
            if j:
                other = after(other, joins[axis])
            column = joined(column, other, (b & t) != 0, axis)
            joins[axis : axis + 1] = [column]
        columns.append(column.reshape(whole, width))

    columns = lax.optimization_barrier(jnp.concatenate(columns, axis=1))
    back = lax.optimization_barrier(matmul(left, columns).astype(low))
    total = matmul_nt(back, right).astype(low)
    update = lax.psum_scatter(total, "dp", scatter_dimension=0, axis_index_groups=[path], tiled=True)
    return (
        jnp.concatenate(first_out, axis=1),
        jnp.concatenate(second_out, axis=1),
        update,
    )


def solution(mesh):
    nb, nd = mesh.shape["basis"], mesh.shape["dp"]

    return jax.shard_map(
        functools.partial(per_device, nb=nb, nd=nd),
        mesh=mesh,
        in_specs=(
            P("basis", "dp"),
            P("basis", "dp"),
            P("basis", "dp"),
            P("basis", "dp"),
            P("basis", "dp"),
        ),
        out_specs=(P("basis", "dp"), P("basis", "dp"), P("dp", "basis")),
        check_vma=False,
    )
```

```python
import functools

import jax
import jax.numpy as jnp
from jax import lax
from jax.experimental import pallas as pl
from jax.experimental.pallas import tpu as pltpu
from jax.sharding import PartitionSpec as P

STEP = 4


beta_first = 0.95
beta_second = 0.95
epsilon = 1e-08

COL_PARTS = 2

VMEM_BYTES = 16 * 1024 * 1024

low = jnp.bfloat16


def matmul(a, b):
    return lax.dot_general(a, b, (((1,), (0,)), ((), ())), preferred_element_type=jnp.float32)


def matmul_nt(a, b):
    return lax.dot_general(a, b, (((1,), (1,)), ((), ())), preferred_element_type=jnp.float32)


def half_rotation(gathered, right, places, nz):
    count, rows, cols = gathered.shape
    nx = count // nz
    width = right.shape[1]

    def kernel(places_ref, gathered_ref, right_ref, out_ref, held, arrived):
        def copies(k):
            return [
                pltpu.make_async_copy(
                    gathered_ref.at[i * nz + (k if i % 2 == 0 else nz - 1 - k)],
                    held.at[k % 2, i],
                    arrived.at[k % 2, i],
                )
                for i in range(nx)
            ]

        for copy in copies(0):
            copy.start()
        for k in range(nz):
            if k + 1 < nz:
                for copy in copies(k + 1):
                    copy.start()
            for copy in copies(k):
                copy.wait()
            total = matmul(held[k % 2, 0], right_ref[:cols])
            for i in range(1, nx):
                total += matmul(held[k % 2, i], right_ref[i * cols : (i + 1) * cols])
            start = pl.multiple_of(places_ref[k] * rows, rows)
            out_ref[pl.ds(start, rows)] = total.astype(out_ref.dtype)

    out = jax.ShapeDtypeStruct((nz * rows, width), low)
    size = sum(a.size * a.dtype.itemsize for a in (gathered, right, out))
    return pl.pallas_call(
        kernel,
        out_shape=out,
        grid_spec=pltpu.PrefetchScalarGridSpec(
            num_scalar_prefetch=1,
            grid=(1,),
            in_specs=[
                pl.BlockSpec(memory_space=pltpu.HBM),
                pl.BlockSpec(right.shape, lambda k, p: (0, 0), pipeline_mode=pl.Buffered(1)),
            ],
            out_specs=pl.BlockSpec(out.shape, lambda k, p: (0, 0)),
            scratch_shapes=[
                pltpu.VMEM((2, nx, rows, cols), gathered.dtype),
                pltpu.SemaphoreType.DMA((2, nx)),
            ],
        ),
        compiler_params=pltpu.CompilerParams(vmem_limit_bytes=VMEM_BYTES),
        cost_estimate=pl.CostEstimate(flops=2 * gathered.size * width, bytes_accessed=size, transcendentals=0),
        name="half_rotation",
    )(places, gathered, right)


def per_device(gradient, left_basis, right_basis, first_moment, second_moment, *, nb, nd):
    nz = nb
    nx = nd // nz
    b = lax.axis_index("basis")
    bits = [1 << k for k in range(nb.bit_length() - 1)]

    def permute(value, target):
        pairs = []
        for bb in range(nb):
            for zz in range(nz):
                for xx in range(nx):
                    tb, tz, tx = target(bb, zz, xx)
                    pairs.append((bb * nd + zz * nx + xx, tb * nd + tz * nx + tx))
        return lax.ppermute(value, ("basis", "dp"), pairs)

    def move_b(value, t):
        return permute(value, lambda bb, zz, xx: (bb ^ t, zz, xx))

    def spread(beta):
        return (beta >> 1) ^ ((beta & 1) * (nz - 1))

    def unspread(w):
        odd = (w >> (len(bits) - 1)) & 1
        return (w ^ (odd * (nz - 1))) * 2 + odd

    def joined(mine, other, bit_set, axis):
        first = jnp.where(bit_set, other, mine)
        second = jnp.where(bit_set, mine, other)
        return jnp.stack([first, second], axis=axis)

    def after(value, *others):
        return lax.optimization_barrier((value,) + others)[0]

    ff_block = right_basis.shape[1]
    rows = first_moment.shape[0]
    out_rows = left_basis.shape[1]
    whole = rows * nb

    path = []
    for xx in range(nx):
        path += [zz * nx + xx for zz in (range(nz) if xx % 2 == 0 else reversed(range(nz)))]

    def reversed_bits(t):
        return sum(((t >> k) & 1) << (len(bits) - 1 - k) for k in range(len(bits)))

    def together(*values):
        return lax.optimization_barrier(values)

    def round_path(value):
        return lax.all_gather(value, "dp", axis_index_groups=[path], tiled=True)

    width = ff_block // COL_PARTS
    right = right_basis.astype(low)
    right_parts = [right_basis[:, j * width : (j + 1) * width].astype(low) for j in range(COL_PARTS)]
    places = jnp.stack([reversed_bits(unspread(b ^ zz) ^ b) for zz in range(nz)]).astype(jnp.int32)

    left_blocks = round_path(left_basis.astype(low).T)
    piece = permute(gradient, lambda bb, zz, xx: (bb, zz ^ spread(bb), xx))
    piece, right_parts, places = together(piece, right_parts, places)
    piece = permute(piece, lambda bb, zz, xx: (zz ^ spread(bb), zz, xx))
    piece, left_blocks = together(piece, left_blocks)
    gathered = round_path(piece)

    left_blocks = left_blocks.reshape(nd, out_rows, rows)
    left_t = jnp.concatenate([left_blocks[path.index(dd)] for dd in range(nd)], axis=0)
    for t in reversed(bits):
        left_t = jnp.concatenate([left_t, move_b(left_t, t)], axis=1)
    left_t, gathered = together(left_t, gathered.reshape(nd, rows, ff_block))

    odd = sorted(range(1, nb, 2), key=lambda t: -t)
    first_group, second_group = odd[: nb // 4], odd[nb // 4 :]
    top = bits[-1]
    last = None

    def paired(t, j):
        nonlocal last
        values = []
        for u in (t, t ^ 1):
            value = half[j] if last is None else after(half[j], last)
            rows_of = lax.dynamic_slice_in_dim(left_t, (b ^ u) * rows, rows, 0)
            last = lax.optimization_barrier(matmul(rows_of, value).astype(low))
            values.append(last)
        return values[1].astype(jnp.float32) + move_b(values[0], 1).astype(jnp.float32)

    half, arrived = [], []
    for j in range(COL_PARTS):
        found = gathered if last is None else after(gathered, last)
        half.append(half_rotation(found, right_parts[j], places, nz))
        away = [lax.optimization_barrier(paired(t, j).astype(low)) for t in first_group]
        last = away[-1]
        if j:
            away = [after(value, arrived[j - 1][-1]) for value in away]
        arrived.append([move_b(value, top) for value in away])
    last = arrived[0][-1]
    sums = []
    for j in range(COL_PARTS):
        held = {t ^ 1: paired(t, j) for t in second_group}
        for t, got in zip(first_group, arrived[j]):
            held[t ^ 1 ^ top] = held[t ^ 1 ^ top] + got.astype(jnp.float32)
        for t in reversed(bits[1:-1]):
            for s in [s for s in held if s & t]:
                held[s ^ t] = held[s ^ t] + move_b(held.pop(s).astype(low), t).astype(jnp.float32)
        sums.append(held[0])

    source = after(left_t, arrived[0][-1])
    left = jnp.concatenate(
        [
            lax.dynamic_slice_in_dim(
                source, reversed_bits(b ^ (dd // nx)) * rows + dd % nx * out_rows, out_rows, 1
            ).T
            for dd in path
        ],
        axis=0,
    )
    left = lax.optimization_barrier(left)

    first_out, second_out, directions = [], [], []
    for j in range(COL_PARTS):
        cols = slice(j * width, (j + 1) * width)
        rotated = sums[j]
        moments = first_moment[:, cols], second_moment[:, cols]
        if j:
            moments = after(moments, directions[-1])
        first_new = beta_first * moments[0] + (1.0 - beta_first) * rotated
        second_new = beta_second * moments[1] + (1.0 - beta_second) * rotated * rotated
        first_fix = 1.0 - beta_first**STEP
        second_fix = 1.0 - beta_second**STEP
        direction = first_new / first_fix / (jnp.sqrt(second_new / second_fix) + epsilon)
        first_out.append(first_new)
        second_out.append(second_new)
        directions.append(direction.astype(low))

    columns, joins = [], []
    for j, column in enumerate(directions):
        for axis, t in enumerate(reversed(bits)):
            other = move_b(column, t)
            if j:
                other = after(other, joins[axis])
            column = joined(column, other, (b & t) != 0, axis)
            joins[axis : axis + 1] = [column]
        columns.append(column.reshape(whole, width))

    columns = lax.optimization_barrier(jnp.concatenate(columns, axis=1))
    back = lax.optimization_barrier(matmul(left, columns).astype(low))
    total = matmul_nt(back, right).astype(low)
    update = lax.psum_scatter(total, "dp", scatter_dimension=0, axis_index_groups=[path], tiled=True)
    return (
        jnp.concatenate(first_out, axis=1),
        jnp.concatenate(second_out, axis=1),
        update,
    )


def solution(mesh):
    nb, nd = mesh.shape["basis"], mesh.shape["dp"]

    return jax.shard_map(
        functools.partial(per_device, nb=nb, nd=nd),
        mesh=mesh,
        in_specs=(
            P("basis", "dp"),
            P("basis", "dp"),
            P("basis", "dp"),
            P("basis", "dp"),
            P("basis", "dp"),
        ),
        out_specs=(P("basis", "dp"), P("basis", "dp"), P("dp", "basis")),
        check_vma=False,
    )
```

```python
import functools

import jax
import jax.numpy as jnp
from jax import lax
from jax.experimental import pallas as pl
from jax.experimental.pallas import tpu as pltpu
from jax.sharding import PartitionSpec as P

STEP = 4


beta_first = 0.95
beta_second = 0.95
epsilon = 1e-08

COL_PARTS = 2

VMEM_BYTES = 52 * 1024 * 1024

low = jnp.bfloat16


def matmul(a, b):
    return lax.dot_general(a, b, (((1,), (0,)), ((), ())), preferred_element_type=jnp.float32)


def matmul_nt(a, b):
    return lax.dot_general(a, b, (((1,), (1,)), ((), ())), preferred_element_type=jnp.float32)


def half_rotation(gathered, right, places, nz):
    count, rows, cols = gathered.shape
    nx = count // nz
    width = right.shape[1]

    def kernel(places_ref, gathered_ref, right_ref, out_ref, held, arrived):
        def copies(k):
            return [
                pltpu.make_async_copy(
                    gathered_ref.at[i * nz + (k if i % 2 == 0 else nz - 1 - k)],
                    held.at[k % 2, i],
                    arrived.at[k % 2, i],
                )
                for i in range(nx)
            ]

        for copy in copies(0):
            copy.start()
        for k in range(nz):
            if k + 1 < nz:
                for copy in copies(k + 1):
                    copy.start()
            for copy in copies(k):
                copy.wait()
            total = matmul(held[k % 2, 0], right_ref[:cols])
            for i in range(1, nx):
                total += matmul(held[k % 2, i], right_ref[i * cols : (i + 1) * cols])
            start = pl.multiple_of(places_ref[k] * rows, rows)
            out_ref[pl.ds(start, rows)] = total.astype(out_ref.dtype)

    out = jax.ShapeDtypeStruct((nz * rows, width), low)
    size = sum(a.size * a.dtype.itemsize for a in (gathered, right, out))
    return pl.pallas_call(
        kernel,
        out_shape=out,
        grid_spec=pltpu.PrefetchScalarGridSpec(
            num_scalar_prefetch=1,
            grid=(1,),
            in_specs=[
                pl.BlockSpec(memory_space=pltpu.HBM),
                pl.BlockSpec(right.shape, lambda k, p: (0, 0), pipeline_mode=pl.Buffered(1)),
            ],
            out_specs=pl.BlockSpec(out.shape, lambda k, p: (0, 0)),
            scratch_shapes=[
                pltpu.VMEM((2, nx, rows, cols), gathered.dtype),
                pltpu.SemaphoreType.DMA((2, nx)),
            ],
        ),
        compiler_params=pltpu.CompilerParams(vmem_limit_bytes=VMEM_BYTES),
        cost_estimate=pl.CostEstimate(flops=2 * gathered.size * width, bytes_accessed=size, transcendentals=0),
        name="half_rotation",
    )(places, gathered, right)


def per_device(gradient, left_basis, right_basis, first_moment, second_moment, *, nb, nd):
    nz = nb
    nx = nd // nz
    b = lax.axis_index("basis")
    bits = [1 << k for k in range(nb.bit_length() - 1)]

    def permute(value, target):
        pairs = []
        for bb in range(nb):
            for zz in range(nz):
                for xx in range(nx):
                    tb, tz, tx = target(bb, zz, xx)
                    pairs.append((bb * nd + zz * nx + xx, tb * nd + tz * nx + tx))
        return lax.ppermute(value, ("basis", "dp"), pairs)

    def move_b(value, t):
        return permute(value, lambda bb, zz, xx: (bb ^ t, zz, xx))

    def spread(beta):
        return (beta >> 1) ^ ((beta & 1) * (nz - 1))

    def unspread(w):
        odd = (w >> (len(bits) - 1)) & 1
        return (w ^ (odd * (nz - 1))) * 2 + odd

    def joined(mine, other, bit_set, axis):
        first = jnp.where(bit_set, other, mine)
        second = jnp.where(bit_set, mine, other)
        return jnp.stack([first, second], axis=axis)

    def after(value, *others):
        return lax.optimization_barrier((value,) + others)[0]

    ff_block = right_basis.shape[1]
    rows = first_moment.shape[0]
    out_rows = left_basis.shape[1]
    whole = rows * nb

    path = []
    for xx in range(nx):
        path += [zz * nx + xx for zz in (range(nz) if xx % 2 == 0 else reversed(range(nz)))]

    def reversed_bits(t):
        return sum(((t >> k) & 1) << (len(bits) - 1 - k) for k in range(len(bits)))

    def together(*values):
        return lax.optimization_barrier(values)

    def round_path(value):
        return lax.all_gather(value, "dp", axis_index_groups=[path], tiled=True)

    width = ff_block // COL_PARTS
    right = right_basis.astype(low)
    right_parts = [right_basis[:, j * width : (j + 1) * width].astype(low) for j in range(COL_PARTS)]
    places = jnp.stack([reversed_bits(unspread(b ^ zz) ^ b) for zz in range(nz)]).astype(jnp.int32)

    left_blocks = round_path(left_basis.astype(low).T)
    piece = permute(gradient, lambda bb, zz, xx: (bb, zz ^ spread(bb), xx))
    piece, right_parts, places = together(piece, right_parts, places)
    piece = permute(piece, lambda bb, zz, xx: (zz ^ spread(bb), zz, xx))
    piece, left_blocks = together(piece, left_blocks)
    gathered = round_path(piece)

    left_blocks = left_blocks.reshape(nd, out_rows, rows)
    left_t = jnp.concatenate([left_blocks[path.index(dd)] for dd in range(nd)], axis=0)
    for t in reversed(bits):
        left_t = jnp.concatenate([left_t, move_b(left_t, t)], axis=1)
    left_t = lax.optimization_barrier(left_t)
    left = jnp.concatenate(
        [
            lax.dynamic_slice_in_dim(
                left_t, reversed_bits(b ^ (dd // nx)) * rows + dd % nx * out_rows, out_rows, 1
            ).T
            for dd in path
        ],
        axis=0,
    )
    left_t, left, gathered = together(left_t, left, gathered.reshape(nd, rows, ff_block))

    odd = sorted(range(1, nb, 2), key=lambda t: -t)
    first_group, second_group = odd[: nb // 4], odd[nb // 4 :]
    top = bits[-1]
    last = None

    def paired(t, j):
        nonlocal last
        values = []
        for u in (t, t ^ 1):
            value = half[j] if last is None else after(half[j], last)
            rows_of = lax.dynamic_slice_in_dim(left_t, (b ^ u) * rows, rows, 0)
            last = lax.optimization_barrier(matmul(rows_of, value).astype(low))
            values.append(last)
        return values[1].astype(jnp.float32) + move_b(values[0], 1).astype(jnp.float32)

    half, arrived = [], []
    for j in range(COL_PARTS):
        found = gathered if last is None else after(gathered, last)
        half.append(half_rotation(found, right_parts[j], places, nz))
        away = [lax.optimization_barrier(paired(t, j).astype(low)) for t in first_group]
        last = away[-1]
        if j:
            away = [after(value, arrived[j - 1][-1]) for value in away]
        arrived.append([move_b(value, top) for value in away])
    last = arrived[0][-1]
    sums = []
    for j in range(COL_PARTS):
        held = {t ^ 1: paired(t, j) for t in second_group}
        for t, got in zip(first_group, arrived[j]):
            held[t ^ 1 ^ top] = held[t ^ 1 ^ top] + got.astype(jnp.float32)
        for t in reversed(bits[1:-1]):
            for s in [s for s in held if s & t]:
                held[s ^ t] = held[s ^ t] + move_b(held.pop(s).astype(low), t).astype(jnp.float32)
        sums.append(held[0])

    first_out, second_out, directions = [], [], []
    for j in range(COL_PARTS):
        cols = slice(j * width, (j + 1) * width)
        rotated = sums[j]
        moments = first_moment[:, cols], second_moment[:, cols]
        if j:
            moments = after(moments, directions[-1])
        first_new = beta_first * moments[0] + (1.0 - beta_first) * rotated
        second_new = beta_second * moments[1] + (1.0 - beta_second) * rotated * rotated
        first_fix = 1.0 - beta_first**STEP
        second_fix = 1.0 - beta_second**STEP
        direction = first_new / first_fix / (jnp.sqrt(second_new / second_fix) + epsilon)
        first_out.append(first_new)
        second_out.append(second_new)
        directions.append(direction.astype(low))

    columns, joins = [], []
    for j, column in enumerate(directions):
        for axis, t in enumerate(reversed(bits)):
            other = move_b(column, t)
            if j:
                other = after(other, joins[axis])
            column = joined(column, other, (b & t) != 0, axis)
            joins[axis : axis + 1] = [column]
        columns.append(column.reshape(whole, width))

    columns = lax.optimization_barrier(jnp.concatenate(columns, axis=1))
    back = lax.optimization_barrier(matmul(left, columns).astype(low))
    total = matmul_nt(back, right).astype(low)
    update = lax.psum_scatter(total, "dp", scatter_dimension=0, axis_index_groups=[path], tiled=True)
    return (
        jnp.concatenate(first_out, axis=1),
        jnp.concatenate(second_out, axis=1),
        update,
    )


def solution(mesh):
    nb, nd = mesh.shape["basis"], mesh.shape["dp"]

    return jax.shard_map(
        functools.partial(per_device, nb=nb, nd=nd),
        mesh=mesh,
        in_specs=(
            P("basis", "dp"),
            P("basis", "dp"),
            P("basis", "dp"),
            P("basis", "dp"),
            P("basis", "dp"),
        ),
        out_specs=(P("basis", "dp"), P("basis", "dp"), P("dp", "basis")),
        check_vma=False,
    )
```

```python
import functools

import jax
import jax.numpy as jnp
from jax import lax
from jax.experimental import pallas as pl
from jax.experimental.pallas import tpu as pltpu
from jax.sharding import PartitionSpec as P

STEP = 4


beta_first = 0.95
beta_second = 0.95
epsilon = 1e-08

COL_PARTS = 2

VMEM_BYTES = 52 * 1024 * 1024

low = jnp.bfloat16


def matmul(a, b):
    return lax.dot_general(a, b, (((1,), (0,)), ((), ())), preferred_element_type=jnp.float32)


def matmul_nt(a, b):
    return lax.dot_general(a, b, (((1,), (1,)), ((), ())), preferred_element_type=jnp.float32)


def half_rotation(gathered, right, places, nz, parts):
    count, rows, cols = gathered.shape
    nx = count // nz
    width = right.shape[1] // parts

    def kernel(places_ref, *refs):
        blocks, right_ref, outs = refs[:nx], refs[nx], refs[nx + 1 :]
        for j, out in enumerate(outs):
            total = matmul(blocks[0][...], right_ref[:cols, j * width : (j + 1) * width])
            for i in range(1, nx):
                total += matmul(blocks[i][...], right_ref[i * cols : (i + 1) * cols, j * width : (j + 1) * width])
            out[...] = total.astype(out.dtype)

    def block_of(i):
        if i % 2 == 0:
            return pl.BlockSpec((None, rows, cols), lambda k, p: (i * nz + k, 0, 0))
        return pl.BlockSpec((None, rows, cols), lambda k, p: (i * nz + nz - 1 - k, 0, 0))

    outs = [jax.ShapeDtypeStruct((nz * rows, width), low)] * parts
    size = sum(a.size * a.dtype.itemsize for a in (gathered, right, *outs))
    return pl.pallas_call(
        kernel,
        out_shape=outs,
        grid_spec=pltpu.PrefetchScalarGridSpec(
            num_scalar_prefetch=1,
            grid=(nz,),
            in_specs=[block_of(i) for i in range(nx)]
            + [pl.BlockSpec(right.shape, lambda k, p: (0, 0), pipeline_mode=pl.Buffered(1))],
            out_specs=[pl.BlockSpec((rows, width), lambda k, p: (p[k], 0))] * parts,
        ),
        compiler_params=pltpu.CompilerParams(vmem_limit_bytes=VMEM_BYTES),
        cost_estimate=pl.CostEstimate(
            flops=2 * gathered.size * right.shape[1], bytes_accessed=size, transcendentals=0
        ),
        name="half_rotation",
    )(places, *([gathered] * nx), right)


def per_device(gradient, left_basis, right_basis, first_moment, second_moment, *, nb, nd):
    nz = nb
    nx = nd // nz
    b = lax.axis_index("basis")
    bits = [1 << k for k in range(nb.bit_length() - 1)]

    def permute(value, target):
        pairs = []
        for bb in range(nb):
            for zz in range(nz):
                for xx in range(nx):
                    tb, tz, tx = target(bb, zz, xx)
                    pairs.append((bb * nd + zz * nx + xx, tb * nd + tz * nx + tx))
        return lax.ppermute(value, ("basis", "dp"), pairs)

    def move_b(value, t):
        return permute(value, lambda bb, zz, xx: (bb ^ t, zz, xx))

    def spread(beta):
        return (beta >> 1) ^ ((beta & 1) * (nz - 1))

    def unspread(w):
        odd = (w >> (len(bits) - 1)) & 1
        return (w ^ (odd * (nz - 1))) * 2 + odd

    def joined(mine, other, bit_set, axis):
        first = jnp.where(bit_set, other, mine)
        second = jnp.where(bit_set, mine, other)
        return jnp.stack([first, second], axis=axis)

    def after(value, *others):
        return lax.optimization_barrier((value,) + others)[0]

    ff_block = right_basis.shape[1]
    rows = first_moment.shape[0]
    out_rows = left_basis.shape[1]
    whole = rows * nb

    path = []
    for xx in range(nx):
        path += [zz * nx + xx for zz in (range(nz) if xx % 2 == 0 else reversed(range(nz)))]

    def reversed_bits(t):
        return sum(((t >> k) & 1) << (len(bits) - 1 - k) for k in range(len(bits)))

    def together(*values):
        return lax.optimization_barrier(values)

    def round_path(value):
        return lax.all_gather(value, "dp", axis_index_groups=[path], tiled=True)

    width = ff_block // COL_PARTS
    right = right_basis.astype(low)
    places = jnp.stack([reversed_bits(unspread(b ^ zz) ^ b) for zz in range(nz)]).astype(jnp.int32)

    left_blocks = round_path(left_basis.astype(low).T)
    piece = permute(gradient, lambda bb, zz, xx: (bb, zz ^ spread(bb), xx))
    piece, right, places = together(piece, right, places)
    piece = permute(piece, lambda bb, zz, xx: (zz ^ spread(bb), zz, xx))
    piece, left_blocks = together(piece, left_blocks)
    gathered = round_path(piece)

    left_blocks = left_blocks.reshape(nd, out_rows, rows)
    left_t = jnp.concatenate([left_blocks[path.index(dd)] for dd in range(nd)], axis=0)
    for t in reversed(bits):
        left_t = jnp.concatenate([left_t, move_b(left_t, t)], axis=1)
    left_t, gathered = together(left_t, gathered.reshape(nd, rows, ff_block))

    odd = sorted(range(1, nb, 2), key=lambda t: -t)
    first_group, second_group = odd[: nb // 4], odd[nb // 4 :]
    top = bits[-1]
    last = None

    def paired(t, j):
        nonlocal last
        values = []
        for u in (t, t ^ 1):
            value = half[j] if last is None else after(half[j], last)
            rows_of = lax.dynamic_slice_in_dim(left_t, (b ^ u) * rows, rows, 0)
            last = lax.optimization_barrier(matmul(rows_of, value).astype(low))
            values.append(last)
        return values[1].astype(jnp.float32) + move_b(values[0], 1).astype(jnp.float32)

    half = half_rotation(gathered, right, places, nz, COL_PARTS)
    arrived = []
    for j in range(COL_PARTS):
        away = [lax.optimization_barrier(paired(t, j).astype(low)) for t in first_group]
        last = away[-1]
        if j:
            away = [after(value, arrived[j - 1][-1]) for value in away]
        arrived.append([move_b(value, top) for value in away])
    last = arrived[0][-1]
    sums = []
    for j in range(COL_PARTS):
        held = {t ^ 1: paired(t, j) for t in second_group}
        for t, got in zip(first_group, arrived[j]):
            held[t ^ 1 ^ top] = held[t ^ 1 ^ top] + got.astype(jnp.float32)
        for t in reversed(bits[1:-1]):
            for s in [s for s in held if s & t]:
                held[s ^ t] = held[s ^ t] + move_b(held.pop(s).astype(low), t).astype(jnp.float32)
        sums.append(held[0])

    source = after(left_t, arrived[0][-1])
    left = jnp.concatenate(
        [
            lax.dynamic_slice_in_dim(
                source, reversed_bits(b ^ (dd // nx)) * rows + dd % nx * out_rows, out_rows, 1
            ).T
            for dd in path
        ],
        axis=0,
    )
    left = lax.optimization_barrier(left)

    first_out, second_out, directions = [], [], []
    for j in range(COL_PARTS):
        cols = slice(j * width, (j + 1) * width)
        rotated = sums[j]
        moments = first_moment[:, cols], second_moment[:, cols]
        if j:
            moments = after(moments, directions[-1])
        first_new = beta_first * moments[0] + (1.0 - beta_first) * rotated
        second_new = beta_second * moments[1] + (1.0 - beta_second) * rotated * rotated
        first_fix = 1.0 - beta_first**STEP
        second_fix = 1.0 - beta_second**STEP
        direction = first_new / first_fix / (jnp.sqrt(second_new / second_fix) + epsilon)
        first_out.append(first_new)
        second_out.append(second_new)
        directions.append(direction.astype(low))

    columns, joins = [], []
    for j, column in enumerate(directions):
        for axis, t in enumerate(reversed(bits)):
            other = move_b(column, t)
            if j:
                other = after(other, joins[axis])
            column = joined(column, other, (b & t) != 0, axis)
            joins[axis : axis + 1] = [column]
        columns.append(column.reshape(whole, width))

    columns = lax.optimization_barrier(jnp.concatenate(columns, axis=1))
    back = lax.optimization_barrier(matmul(left, columns).astype(low))
    total = matmul_nt(back, right).astype(low)
    update = lax.psum_scatter(total, "dp", scatter_dimension=0, axis_index_groups=[path], tiled=True)
    return (
        jnp.concatenate(first_out, axis=1),
        jnp.concatenate(second_out, axis=1),
        update,
    )


def solution(mesh):
    nb, nd = mesh.shape["basis"], mesh.shape["dp"]

    return jax.shard_map(
        functools.partial(per_device, nb=nb, nd=nd),
        mesh=mesh,
        in_specs=(
            P("basis", "dp"),
            P("basis", "dp"),
            P("basis", "dp"),
            P("basis", "dp"),
            P("basis", "dp"),
        ),
        out_specs=(P("basis", "dp"), P("basis", "dp"), P("dp", "basis")),
        check_vma=False,
    )
```

```python
import functools

import jax
import jax.numpy as jnp
from jax import lax
from jax.experimental import pallas as pl
from jax.experimental.pallas import tpu as pltpu
from jax.sharding import PartitionSpec as P

STEP = 4


beta_first = 0.95
beta_second = 0.95
epsilon = 1e-08

COL_PARTS = 2

VMEM_BYTES = 20 * 1024 * 1024

low = jnp.bfloat16


def matmul(a, b):
    return lax.dot_general(a, b, (((1,), (0,)), ((), ())), preferred_element_type=jnp.float32)


def matmul_nt(a, b):
    return lax.dot_general(a, b, (((1,), (1,)), ((), ())), preferred_element_type=jnp.float32)


def half_rotation(gathered, right, places, nz, parts):
    count, rows, cols = gathered.shape
    nx = count // nz
    width = right.shape[1] // parts

    def kernel(places_ref, *refs):
        blocks, right_ref, outs = refs[:nx], refs[nx], refs[nx + 1 :]
        for j, out in enumerate(outs):
            total = matmul(blocks[0][...], right_ref[:cols, j * width : (j + 1) * width])
            for i in range(1, nx):
                total += matmul(blocks[i][...], right_ref[i * cols : (i + 1) * cols, j * width : (j + 1) * width])
            out[...] = total.astype(out.dtype)

    def block_of(i):
        if i % 2 == 0:
            return pl.BlockSpec((None, rows, cols), lambda k, p: (i * nz + k, 0, 0))
        return pl.BlockSpec((None, rows, cols), lambda k, p: (i * nz + nz - 1 - k, 0, 0))

    outs = [jax.ShapeDtypeStruct((nz * rows, width), low)] * parts
    size = sum(a.size * a.dtype.itemsize for a in (gathered, right, *outs))
    return pl.pallas_call(
        kernel,
        out_shape=outs,
        grid_spec=pltpu.PrefetchScalarGridSpec(
            num_scalar_prefetch=1,
            grid=(nz,),
            in_specs=[block_of(i) for i in range(nx)]
            + [pl.BlockSpec(right.shape, lambda k, p: (0, 0), pipeline_mode=pl.Buffered(1))],
            out_specs=[pl.BlockSpec((rows, width), lambda k, p: (p[k], 0))] * parts,
        ),
        compiler_params=pltpu.CompilerParams(vmem_limit_bytes=VMEM_BYTES),
        cost_estimate=pl.CostEstimate(
            flops=2 * gathered.size * right.shape[1], bytes_accessed=size, transcendentals=0
        ),
        name="half_rotation",
    )(places, *([gathered] * nx), right)


def per_device(gradient, left_basis, right_basis, first_moment, second_moment, *, nb, nd):
    nz = nb
    nx = nd // nz
    b = lax.axis_index("basis")
    bits = [1 << k for k in range(nb.bit_length() - 1)]

    def permute(value, target):
        pairs = []
        for bb in range(nb):
            for zz in range(nz):
                for xx in range(nx):
                    tb, tz, tx = target(bb, zz, xx)
                    pairs.append((bb * nd + zz * nx + xx, tb * nd + tz * nx + tx))
        return lax.ppermute(value, ("basis", "dp"), pairs)

    def move_b(value, t):
        return permute(value, lambda bb, zz, xx: (bb ^ t, zz, xx))

    def spread(beta):
        return (beta >> 1) ^ ((beta & 1) * (nz - 1))

    def unspread(w):
        odd = (w >> (len(bits) - 1)) & 1
        return (w ^ (odd * (nz - 1))) * 2 + odd

    def joined(mine, other, bit_set, axis):
        first = jnp.where(bit_set, other, mine)
        second = jnp.where(bit_set, mine, other)
        return jnp.stack([first, second], axis=axis)

    def after(value, *others):
        return lax.optimization_barrier((value,) + others)[0]

    ff_block = right_basis.shape[1]
    rows = first_moment.shape[0]
    out_rows = left_basis.shape[1]
    whole = rows * nb

    path = []
    for xx in range(nx):
        path += [zz * nx + xx for zz in (range(nz) if xx % 2 == 0 else reversed(range(nz)))]

    def reversed_bits(t):
        return sum(((t >> k) & 1) << (len(bits) - 1 - k) for k in range(len(bits)))

    def together(*values):
        return lax.optimization_barrier(values)

    def round_path(value):
        return lax.all_gather(value, "dp", axis_index_groups=[path], tiled=True)

    width = ff_block // COL_PARTS
    right = right_basis.astype(low)
    places = jnp.stack([reversed_bits(unspread(b ^ zz) ^ b) for zz in range(nz)]).astype(jnp.int32)

    left_blocks = round_path(left_basis.astype(low).T)
    piece = permute(gradient, lambda bb, zz, xx: (bb, zz ^ spread(bb), xx))
    piece, right, places = together(piece, right, places)
    piece = permute(piece, lambda bb, zz, xx: (zz ^ spread(bb), zz, xx))
    piece, left_blocks = together(piece, left_blocks)
    gathered = round_path(piece)

    left_blocks = left_blocks.reshape(nd, out_rows, rows)
    left_t = jnp.concatenate([left_blocks[path.index(dd)] for dd in range(nd)], axis=0)
    for t in reversed(bits):
        left_t = jnp.concatenate([left_t, move_b(left_t, t)], axis=1)
    left_t, gathered = together(left_t, gathered.reshape(nd, rows, ff_block))

    odd = sorted(range(1, nb, 2), key=lambda t: -t)
    first_group, second_group = odd[: nb // 4], odd[nb // 4 :]
    top = bits[-1]
    last = None

    def paired(t, j):
        nonlocal last
        values = []
        for u in (t, t ^ 1):
            value = half[j] if last is None else after(half[j], last)
            rows_of = lax.dynamic_slice_in_dim(left_t, (b ^ u) * rows, rows, 0)
            last = lax.optimization_barrier(matmul(rows_of, value).astype(low))
            values.append(last)
        return values[1].astype(jnp.float32) + move_b(values[0], 1).astype(jnp.float32)

    half = half_rotation(gathered, right, places, nz, COL_PARTS)
    arrived = []
    for j in range(COL_PARTS):
        away = [lax.optimization_barrier(paired(t, j).astype(low)) for t in first_group]
        last = away[-1]
        if j:
            away = [after(value, arrived[j - 1][-1]) for value in away]
        arrived.append([move_b(value, top) for value in away])
    sums = []
    for j in range(COL_PARTS):
        held = {t ^ 1: paired(t, j) for t in second_group}
        for t, got in zip(first_group, arrived[j]):
            held[t ^ 1 ^ top] = held[t ^ 1 ^ top] + got.astype(jnp.float32)
        for t in reversed(bits[1:-1]):
            for s in [s for s in held if s & t]:
                held[s ^ t] = held[s ^ t] + move_b(held.pop(s).astype(low), t).astype(jnp.float32)
        sums.append(held[0])

    source = after(left_t, arrived[0][-1])
    left = jnp.concatenate(
        [
            lax.dynamic_slice_in_dim(
                source, reversed_bits(b ^ (dd // nx)) * rows + dd % nx * out_rows, out_rows, 1
            ).T
            for dd in path
        ],
        axis=0,
    )
    left = lax.optimization_barrier(left)

    first_out, second_out, directions = [], [], []
    for j in range(COL_PARTS):
        cols = slice(j * width, (j + 1) * width)
        rotated = sums[j]
        moments = first_moment[:, cols], second_moment[:, cols]
        if j:
            moments = after(moments, directions[-1])
        first_new = beta_first * moments[0] + (1.0 - beta_first) * rotated
        second_new = beta_second * moments[1] + (1.0 - beta_second) * rotated * rotated
        first_fix = 1.0 - beta_first**STEP
        second_fix = 1.0 - beta_second**STEP
        direction = first_new / first_fix / (jnp.sqrt(second_new / second_fix) + epsilon)
        first_out.append(first_new)
        second_out.append(second_new)
        directions.append(direction.astype(low))

    columns, joins = [], []
    for j, column in enumerate(directions):
        for axis, t in enumerate(reversed(bits)):
            other = move_b(column, t)
            if j:
                other = after(other, joins[axis])
            column = joined(column, other, (b & t) != 0, axis)
            joins[axis : axis + 1] = [column]
        columns.append(column.reshape(whole, width))

    columns = lax.optimization_barrier(jnp.concatenate(columns, axis=1))
    back = lax.optimization_barrier(matmul(left, columns).astype(low))
    total = matmul_nt(back, right).astype(low)
    update = lax.psum_scatter(total, "dp", scatter_dimension=0, axis_index_groups=[path], tiled=True)
    return (
        jnp.concatenate(first_out, axis=1),
        jnp.concatenate(second_out, axis=1),
        update,
    )


def solution(mesh):
    nb, nd = mesh.shape["basis"], mesh.shape["dp"]

    return jax.shard_map(
        functools.partial(per_device, nb=nb, nd=nd),
        mesh=mesh,
        in_specs=(
            P("basis", "dp"),
            P("basis", "dp"),
            P("basis", "dp"),
            P("basis", "dp"),
            P("basis", "dp"),
        ),
        out_specs=(P("basis", "dp"), P("basis", "dp"), P("dp", "basis")),
        check_vma=False,
    )
```
